256 devices in a mesh: subdomai: 8 (over x, core), inner: 32 (over z, y).
Axes of the slice: x: 4, y: 4, z: 8, core: 2. Of those that a mesh axis runs over, the one named last changes fastest.
Arguments:
- start_vectors: float32 [8, 4096, 64, 128], P(None, ('subdomai', 'inner')), may hold values from -6 to 6
- permeability: float32 [4096, 64, 128], P(('subdomai', 'inner')), may hold values from 0.01 to 100
- accumulation: float32 [4096, 64, 128], P(('subdomai', 'inner')), may hold values from 0.1 to 2
- extents: int32 [8, 2], P('subdomai'), may hold values from 2 to 512, as said below
- neighbour_ids: int32 [8, 6], P('subdomai'), may hold values from 0 to 7, as said below
- intersection_widths: int32 [8, 6], P('subdomai'), may hold values from 1 to 4, as said below
Outputs:
- coarse_basis: float32 [8, 4096, 64, 128], P(None, ('subdomai', 'inner'))
- galerkin: float32 [8, 8, 8], P('subdomai')
- coupling: float32 [8, 6, 8, 8], P('subdomai')
The draws below stay inside these ranges and needn't reach their ends.
Inputs may be any that keep to these rules, and one draw needn't show every extreme that they name: extents[i] = (first-dimension extent in 2 to 512, third-dimension extent in 4 to 128); in every draw some subdomain is active in full. `neighbour_ids`: each row lists 6 different subdomains other than its own. `intersection_widths`: 4 is reached in every draw.
All inputs are finite; a program needn't handle non-finite values.
Results may differ from the reference program's by a relative error of at most 0.0003.
Values sent between devices are 32-bit elements; how exact they have to be, the bound alone decides.
No kernel may reach another device: no remote copies, remote signals or barrier semaphores. Data moves between devices by JAX's collectives and lax.ppermute only.
A program may use at most 192 MiB of HBM per device.

```python
import math
import jax
import jax.numpy as jnp
from jax import lax

K = 8
NB = 6
WMAX = 4
ITERS = 2
CY = 64
CZ = 128
SUBDOMAINS = 8
NXS = 512
CELLS = 4194304
NXALL = 4096


def draw_extents(key, part):
    key = jax.random.fold_in(key, 11)
    key_x, key_z, key_pick = jax.random.split(key, 3)
    across = jax.random.randint(key_x, (SUBDOMAINS,), 2, NXS + 1)
    depths = jax.random.randint(key_z, (SUBDOMAINS,), WMAX, CZ + 1)
    chosen_row = jax.random.randint(key_pick, (), 0, SUBDOMAINS)
    filled = jnp.arange(SUBDOMAINS) == chosen_row
    across = jnp.where(filled, NXS, across)
    depths = jnp.where(filled, CZ, depths)
    return jnp.stack([across, depths], axis=1).astype(jnp.int32)


def draw_neighbour_ids(key, part):
    key = jax.random.fold_in(key, 12)
    row_keys = jax.random.split(key, SUBDOMAINS)

    def one_row(row_key, row):
        offsets = jax.random.permutation(row_key, SUBDOMAINS - 1)[:NB] + 1
        return (row + offsets) % SUBDOMAINS
    return jax.vmap(one_row)(row_keys, jnp.arange(SUBDOMAINS)).astype(jnp.int32)


def draw_intersection_widths(key, part):
    key = jax.random.fold_in(key, 13)
    key_w, key_pick = jax.random.split(key)
    widths = jax.random.randint(key_w, (SUBDOMAINS * NB,), 1, WMAX + 1)
    chosen_entry = jax.random.randint(key_pick, (), 0, SUBDOMAINS * NB)
    widths = jnp.where(jnp.arange(SUBDOMAINS * NB) == chosen_entry, WMAX, widths)
    return widths.reshape(SUBDOMAINS, NB).astype(jnp.int32)


def steps_of(rng, dims, pieces, smallest, largest):
    def one(dim, shards_of):
        steps = jax.random.uniform(jax.random.fold_in(jax.random.fold_in(rng, 6), dim), (shards_of,), jnp.float32, smallest / len(pieces), largest / len(pieces))
        return jnp.repeat(jnp.exp(steps), dims[dim] // shards_of).reshape((-1,) + (1,) * (len(dims) - dim - 1))

    gain = one(*pieces[0])
    for cut in pieces[1:]:
        gain = gain * one(*cut)
    return gain


def noise(own_key, dims, width, bound, shards=(), kind=jnp.bfloat16):
    gain = steps_of(own_key, dims, shards, -0.22, 0.18) if shards else 1.0
    result = jax.random.normal(own_key, dims, jnp.float32) * width * gain
    return jnp.minimum(jnp.maximum(result, -bound), bound).astype(kind)


def setup_inputs(seed: int = 0) -> dict:
    keys = jax.random.split(jax.random.key(seed), 7)
    return {
        "start_vectors": noise(keys[0], (K, NXALL, CY, CZ), 1.0, 6.0, ((1, 256),), jnp.float32),
        "permeability": jnp.clip(jnp.exp(math.log(100.0) - 9.2103404 * jax.random.uniform(keys[1], (NXALL, CY, CZ), jnp.float32) ** steps_of(keys[1], (NXALL, CY, CZ), ((0, 256),), -0.2, 0.2)), 0.01, 100.0),
        "accumulation": jnp.clip(jnp.exp(math.log(2.0) - 2.9957323 * jax.random.uniform(keys[2], (NXALL, CY, CZ), jnp.float32) ** steps_of(keys[2], (NXALL, CY, CZ), ((0, 256),), -0.2, 0.2)), 0.1, 2.0),
        "extents": draw_extents(jax.random.fold_in(keys[6], 71), 0),
        "neighbour_ids": draw_neighbour_ids(jax.random.fold_in(keys[6], 71), 0),
        "intersection_widths": draw_intersection_widths(jax.random.fold_in(keys[6], 71), 0),
    }


omega = 0.6

def face_terms(perm_pad, mask_pad, axis):
    count = perm_pad.shape[axis]
    first = lax.slice_in_dim(perm_pad, 0, count - 1, axis=axis)
    second = lax.slice_in_dim(perm_pad, 1, count, axis=axis)
    mfirst = lax.slice_in_dim(mask_pad, 0, count - 1, axis=axis)
    msecond = lax.slice_in_dim(mask_pad, 1, count, axis=axis)
    return mfirst * msecond * 2.0 * first * second / (first + second)

def coefficients(perm_xpad, mask_xpad, accum):
    perm = perm_xpad[1:-1]
    mask = mask_xpad[1:-1]
    along_x = face_terms(perm_xpad, mask_xpad, 0)
    along_y = face_terms(jnp.pad(perm, ((0, 0), (1, 1), (0, 0))), jnp.pad(mask, ((0, 0), (1, 1), (0, 0))), 1)
    along_z = face_terms(jnp.pad(perm, ((0, 0), (0, 0), (1, 1))), jnp.pad(mask, ((0, 0), (0, 0), (1, 1))), 2)
    diagonal = accum + along_x[1:] + along_x[:-1] + along_y[:, 1:] + along_y[:, :-1] + along_z[:, :, 1:] + along_z[:, :, :-1]
    return (along_x, along_y, along_z, diagonal, accum)

def apply_flux(field, field_xpad, terms):
    along_x, along_y, along_z, diagonal, accum = terms
    flux = along_x[1:] * (field - field_xpad[:, 2:]) + along_x[:-1] * (field - field_xpad[:, :-2])
    ypad = jnp.pad(field, ((0, 0), (0, 0), (1, 1), (0, 0)))
    flux = flux + along_y[:, 1:] * (field - ypad[:, :, 2:]) + along_y[:, :-1] * (field - ypad[:, :, :-2])
    zpad = jnp.pad(field, ((0, 0), (0, 0), (0, 0), (1, 1)))
    flux = flux + along_z[:, :, 1:] * (field - zpad[:, :, :, 2:]) + along_z[:, :, :-1] * (field - zpad[:, :, :, :-2])
    return accum * field + flux

def inner_product(left, right):
    return jnp.einsum('axyz,bxyz->ab', left, right, precision=lax.Precision.HIGHEST)

def inverse_factor(gram):
    lower = jnp.linalg.cholesky(gram)
    eye_matrix = jnp.eye(gram.shape[0], dtype=gram.dtype)
    return lax.linalg.triangular_solve(lower, eye_matrix, left_side=True, lower=True)

def active_mask(x_index, ex_limit, ez_limit, ny_count, nz_count):
    inside_x = (x_index >= 0) & (x_index < ex_limit)
    inside_z = jnp.arange(nz_count, dtype=jnp.int32) < ez_limit
    joined = inside_x[:, None, None] & inside_z[None, None, :]
    return jnp.broadcast_to(joined, (x_index.shape[0], ny_count, nz_count)).astype(jnp.float32)

def selector(ez_limit, widths, nz_count, wmax):
    depth = jnp.arange(nz_count, dtype=jnp.int32)[None, :, None]
    layer = jnp.arange(wmax, dtype=jnp.int32)[None, None, :]
    wide = widths[:, None, None]
    return ((depth == ez_limit - wide + layer) & (layer < wide)).astype(jnp.float32)

def first_layers(field, wmax):
    count, nx_count, ny_count, nz_count = field.shape
    return field.reshape(count, nx_count * ny_count, nz_count)[:, :, :wmax].transpose(0, 2, 1)

def weighted_layers(field, perm, ez_limit, widths, wmax):
    count, nx_count, ny_count, nz_count = field.shape
    chosen = selector(ez_limit, widths, nz_count, wmax)
    scaled = (field * perm).reshape(count, nx_count * ny_count, nz_count)
    return jnp.einsum('apz,nzt->natp', scaled, chosen, precision=lax.Precision.HIGHEST)

def reference(start_vectors, permeability, accumulation, extents, neighbour_ids, intersection_widths):
    starts = start_vectors.reshape(K, SUBDOMAINS, NXS, CY, CZ).transpose(1, 0, 2, 3, 4)
    perms = permeability.reshape(SUBDOMAINS, NXS, CY, CZ)
    accums = accumulation.reshape(SUBDOMAINS, NXS, CY, CZ)

    def local(item):
        start, perm, accum, extent = item
        x_index = jnp.arange(NXS + 2, dtype=jnp.int32) - 1
        mask_xpad = active_mask(x_index, extent[0], extent[1], CY, CZ)
        perm_xpad = jnp.pad(perm, ((1, 1), (0, 0), (0, 0)))
        terms = coefficients(perm_xpad, mask_xpad, accum)
        basis = start * mask_xpad[1:-1]
        for step in range(ITERS):
            image = apply_flux(basis, jnp.pad(basis, ((0, 0), (1, 1), (0, 0), (0, 0))), terms)
            basis = basis - omega * image / terms[3]
        gram = inner_product(basis, basis) / CELLS
        basis = jnp.einsum('ab,bxyz->axyz', inverse_factor(gram), basis, precision=lax.Precision.HIGHEST)
        image = apply_flux(basis, jnp.pad(basis, ((0, 0), (1, 1), (0, 0), (0, 0))), terms)
        projected = inner_product(basis, image) / CELLS
        return (basis, projected, first_layers(basis, WMAX))
    bases, galerkin, layers = lax.map(local, (starts, perms, accums, extents))

    def couple(item):
        basis, perm, extent, neighbours, widths = item
        own = weighted_layers(basis, perm, extent[1], widths, WMAX)
        other = layers[neighbours]
        return jnp.einsum('natp,nbtp->nab', own, other, precision=lax.Precision.HIGHEST) / CELLS
    coupling = lax.map(couple, (bases, perms, extents, neighbour_ids, intersection_widths))
    coarse_basis = bases.transpose(1, 0, 2, 3, 4).reshape(K, SUBDOMAINS * NXS, CY, CZ)
    return (coarse_basis, galerkin, coupling)
```

```python
import functools
import jax
import jax.numpy as jnp
from jax import lax
from jax.experimental import pallas as pl
from jax.experimental.pallas import tpu as pltpu
from jax.sharding import PartitionSpec as P

F32 = jnp.float32
K = 8
NB = 6
WMAX = 4
CY = 64
CZ = 128
OMEGA = 0.6
SLAB = 16 * CY
HALO = 160
HALO_ACC = 96
OFF = HALO + 8
RT = SLAB + 2 * OFF
PACK = K * HALO + HALO + HALO_ACC
PAIRS = [(a, b) for b in range(K) for a in range(b + 1)]
NP = len(PAIRS)
HIGHEST = lax.Precision.HIGHEST
VMEM = pl.BlockSpec(memory_space=pltpu.VMEM)
SMEM = pl.BlockSpec(memory_space=pltpu.SMEM)
ANY = pl.BlockSpec(memory_space=pl.ANY)


def shape(*dims):
    return jax.ShapeDtypeStruct(dims, F32)


def rows_loop(lo, hi, step, init=(), tiles=4):
    def one(i, carry):
        stores = []
        for j in range(tiles):
            more, carry = step(pl.multiple_of(lo + OFF + (i * tiles + j) * 8, 8), carry)
            stores += more
        for ref, place, value in stores:
            ref[place] = value
        return carry

    assert (hi - lo) % (8 * tiles) == 0
    return lax.fori_loop(0, (hi - lo) // (8 * tiles), one, init)


def tile_at(row):
    return (pl.ds(row, 8), slice(None))


def field_at(a, row):
    return (a, pl.ds(row, 8), slice(None))


def lanes():
    return lax.broadcasted_iota(jnp.int32, (8, CZ), 1)


def sublanes():
    return lax.broadcasted_iota(jnp.int32, (8, CZ), 0)


def at(ref, row):
    return ref[pl.ds(row, 8), :]


def fat(ref, a, row):
    return ref[a, pl.ds(row, 8), :]


def layer_of(row):
    return lax.shift_right_arithmetic(row + (192 - OFF), 6) - 3


def active(scal, row, more=0):
    x = scal[2] + layer_of(row) + more
    return jnp.where((x >= 0) & (x < scal[0]), 1.0, 0.0).astype(F32)


def faces(scal, kp, fx, fy, fz, lo, hi):
    mz = jnp.where(lanes() < scal[1], 2.0, 0.0).astype(F32)
    mzz = jnp.where(lanes() < scal[1] - 1, 2.0, 0.0).astype(F32)
    sub = sublanes()

    def step(r, carry):
        here = active(scal, r)
        there = active(scal, r, 1)
        k = at(kp, r)
        kx = at(kp, r + CY)
        ky = at(kp, r + 1)
        kz = pltpu.roll(k, CZ - 1, 1)
        inside = jnp.where(((r + (192 - OFF)) & (CY - 1)) == CY - 8, 0.0, 1.0).astype(F32)
        my = jnp.where(sub == 7, inside, 1.0)
        stores = [
            (fx, tile_at(r), (mz * (here * there)) * k * kx / (k + kx)),
            (fy, tile_at(r), (mz * here) * my * k * ky / (k + ky)),
            (fz, tile_at(r), (mzz * here) * k * kz / (k + kz)),
        ]
        return stores, carry

    rows_loop(lo, hi, step)


def weights(ac, fx, fy, fz, w, lo, hi):
    def step(r, carry):
        z = at(fz, r)
        diagonal = (
            (at(ac, r) + at(fx, r))
            + (at(fx, r - CY) + at(fy, r))
            + (at(fy, r - 1) + z)
            + pltpu.roll(z, 1, 1)
        )
        return [(w, tile_at(r), OMEGA / diagonal)], carry

    rows_loop(lo, hi, step)


def smooth(scal, src, dst, fx, fy, fz, w, lo, hi, masked):
    mz = jnp.where(lanes() < scal[1], 1.0 - OMEGA, 0.0).astype(F32)

    def step(r, carry):
        wt = at(w, r)
        z = at(fz, r)
        xp = wt * at(fx, r)
        xm = wt * at(fx, r - CY)
        yp = wt * at(fy, r)
        ym = wt * at(fy, r - 1)
        zp = wt * z
        zm = wt * pltpu.roll(z, 1, 1)
        centre = mz * active(scal, r) if masked else 1.0 - OMEGA
        stores = []
        for a in range(K):
            v = fat(src, a, r)
            new = (
                (centre * v + xp * fat(src, a, r + CY))
                + (xm * fat(src, a, r - CY) + yp * fat(src, a, r + 1))
                + (ym * fat(src, a, r - 1) + zp * pltpu.roll(v, CZ - 1, 1))
                + zm * pltpu.roll(v, 1, 1)
            )
            stores.append((dst, field_at(a, r), new))
        return stores, carry

    rows_loop(lo, hi, step)


def gram_sums(s, lo, hi, acc):
    def step(r, acc):
        v = [fat(s, a, r) for a in range(K)]
        return [], tuple(t + v[a] * v[b] for t, (a, b) in zip(acc, PAIRS))

    return rows_loop(lo, hi, step, tuple(acc), tiles=2)


def flux_sums(s, ac, fx, fy, fz, lo, hi, acc, before=True, after=True):
    def step(r, acc):
        out = list(acc)
        z = at(fz, r)
        xp = at(fx, r)
        xm = at(fx, r - CY)
        yp = at(fy, r)
        ym = at(fy, r - 1)
        d = at(ac, r)
        v = [fat(s, a, r) for a in range(K)]
        g = [c - pltpu.roll(c, CZ - 1, 1) for c in v]
        for b in range(K):
            c = v[b]
            image = d * c + yp * (c - fat(s, b, r + 1)) + ym * (c - fat(s, b, r - 1))
            if after:
                image = image + xp * (c - fat(s, b, r + CY))
            if before:
                image = image + xm * (c - fat(s, b, r - CY))
            slope = z * g[b]
            for a in range(b + 1):
                p = b * (b + 1) // 2 + a
                out[p] = out[p] + (v[a] * image + g[a] * slope)
        return [], tuple(out)

    return rows_loop(lo, hi, step, tuple(acc), tiles=1)


def crossing_sums(s, fx, lo, hi, acc):
    def step(r, acc):
        f = at(fx, r)
        d = [fat(s, a, r) - fat(s, a, r + CY) for a in range(K)]
        e = [f * t for t in d]
        return [], tuple(t + d[a] * e[b] for t, (a, b) in zip(acc, PAIRS))

    return rows_loop(lo, hi, step, tuple(acc), tiles=1)


def turned(scal, s, kp, first, window, tile, ptile, blocks):
    start = scal[1] - WMAX

    def step(block, row, lane):
        ptile[...] = kp[pl.ds(row, CZ), :].T
        kw = ptile[pl.ds(start, WMAX), :]
        for a in range(K):
            tile[a] = s[a, pl.ds(row, CZ), :].T
        for a in range(K):
            u = tile[a, pl.ds(start, WMAX), :] * kw
            f = tile[a, pl.ds(0, WMAX), :]
            for t in range(WMAX):
                first[pl.ds(t * K + a, 1), pl.ds(lane, CZ)] = f[t : t + 1]
                window[pl.ds(t * K + a, 1), pl.ds(lane, CZ)] = u[t : t + 1]

    def one(block, carry):
        step(block, pl.multiple_of(OFF + block * CZ, 8), pl.multiple_of((block - blocks[0]) * CZ, CZ))
        return carry

    lax.fori_loop(blocks[0], blocks[1], one, 0)


def copy_all(pairs, sem):
    copies = [pltpu.make_async_copy(src, dst, sem.at[i]) for i, (src, dst) in enumerate(pairs)]
    for c in copies:
        c.start()
    return copies


def wait_all(copies):
    for c in copies:
        c.wait()


def pack_kernel(sv, perm, acc, down, up, sem):
    pairs = []
    for out, lo, acc_lo in ((down, 0, 0), (up, SLAB - HALO, SLAB - HALO_ACC)):
        for a in range(K):
            pairs.append((sv.at[a, pl.ds(lo, HALO)], out.at[pl.ds(a * HALO, HALO)]))
        pairs.append((perm.at[pl.ds(lo, HALO)], out.at[pl.ds(K * HALO, HALO)]))
        pairs.append((acc.at[pl.ds(acc_lo, HALO_ACC)], out.at[pl.ds((K + 1) * HALO, HALO_ACC)]))
    wait_all(copy_all(pairs, sem))


INSIDE = SLAB - 4 * CY


def interior_kernel(
    scal, sv, perm, acc, si, ve, gram, flux, first, window, v0, v1, s, kp, ac, fx, fy, fz, w, tile, ptile, sem
):
    slab = pl.ds(OFF, SLAB)
    a, b, c = copy_all([(perm, kp.at[slab]), (acc, ac.at[slab]), (sv, v0.at[:, slab])], sem)
    a.wait()
    faces(scal, kp, fx, fy, fz, 0, SLAB - CY)
    b.wait()
    weights(ac, fx, fy, fz, w, CY, SLAB - CY)
    c.wait()
    smooth(scal, v0, v1, fx, fy, fz, w, CY, SLAB - CY, True)
    smooth(scal, v1, s, fx, fy, fz, w, 2 * CY, SLAB - 2 * CY, False)
    out = copy_all(
        [
            (s.at[:, pl.ds(OFF + 2 * CY, INSIDE)], si),
            (v1.at[:, pl.ds(OFF + CY, CZ)], ve.at[0]),
            (v1.at[:, pl.ds(OFF + SLAB - CY - CZ, CZ)], ve.at[1]),
        ],
        sem,
    )
    zero = [jnp.zeros((8, CZ), F32)] * NP
    for i, t in enumerate(gram_sums(s, 2 * CY, SLAB - 2 * CY, zero)):
        gram[i] = t
    for i, t in enumerate(flux_sums(s, ac, fx, fy, fz, 3 * CY, SLAB - 3 * CY, zero)):
        flux[i] = t
    turned(scal, s, kp, first, window, tile, ptile, (1, 7))
    wait_all(out)


def edge_kernel(
    scal, left, right, sv, perm, acc, si, ve, gram, flux, firsti, windowi,
    se, first, window, part, v0, v1, s, kp, ac, fx, fy, fz, w, fe, we, tile, ptile, sem,
):
    pairs = []
    far = SLAB - 2 * CZ
    for src, lo, acc_lo, near in ((left, -HALO, -HALO_ACC, 0), (right, SLAB, SLAB, far)):
        pairs.append((src.at[pl.ds(K * HALO, HALO)], kp.at[pl.ds(OFF + lo, HALO)]))
        pairs.append((src.at[pl.ds((K + 1) * HALO, HALO_ACC)], ac.at[pl.ds(OFF + acc_lo, HALO_ACC)]))
        for a in range(K):
            pairs.append((src.at[pl.ds(a * HALO, HALO)], v0.at[a, pl.ds(OFF + lo, HALO)]))
        pairs.append((perm.at[pl.ds(near, 2 * CZ)], kp.at[pl.ds(OFF + near, 2 * CZ)]))
        pairs.append((acc.at[pl.ds(near, 2 * CZ)], ac.at[pl.ds(OFF + near, 2 * CZ)]))
        pairs.append((sv.at[:, pl.ds(near, 2 * CZ)], v0.at[:, pl.ds(OFF + near, 2 * CZ)]))
    pairs.append((ve.at[0], v1.at[:, pl.ds(OFF + CY, CZ)]))
    pairs.append((ve.at[1], v1.at[:, pl.ds(OFF + SLAB - CY - CZ, CZ)]))
    pairs.append((si.at[:, pl.ds(0, CZ)], s.at[:, pl.ds(OFF + CZ, CZ)]))
    pairs.append((si.at[:, pl.ds(INSIDE - CZ, CZ)], s.at[:, pl.ds(OFF + SLAB - 2 * CZ, CZ)]))
    wait_all(copy_all(pairs, sem))
    faces(scal, kp, fx, fy, fz, -HALO, 3 * CY)
    faces(scal, kp, fx, fy, fz, SLAB - 4 * CY, SLAB + HALO_ACC)
    weights(ac, fx, fy, fz, w, -HALO_ACC, 2 * CY)
    weights(ac, fx, fy, fz, w, SLAB - 2 * CY, SLAB + HALO_ACC)
    smooth(scal, v0, v1, fx, fy, fz, w, -HALO_ACC, CY, True)
    smooth(scal, v0, v1, fx, fy, fz, w, SLAB - CY, SLAB + HALO_ACC, True)
    smooth(scal, v1, s, fx, fy, fz, w, -32, 2 * CY, False)
    smooth(scal, v1, s, fx, fy, fz, w, SLAB - 2 * CY, SLAB + 32, False)
    out = copy_all(
        [
            (s.at[:, pl.ds(OFF, CZ)], se.at[0]),
            (s.at[:, pl.ds(OFF + SLAB - CZ, CZ)], se.at[1]),
        ],
        sem,
    )
    for whole, inside in ((first, firsti), (window, windowi)):
        whole[:, pl.ds(CZ, INSIDE)] = inside[...]
    for i, lane in ((0, 0), (7, SLAB - CZ)):
        turned(scal, s, kp, fe, we, tile, ptile, (i, i + 1))
        first[:, pl.ds(lane, CZ)] = fe[...]
        window[:, pl.ds(lane, CZ)] = we[...]
    acc = [gram[i] for i in range(NP)]
    acc = gram_sums(s, 0, 2 * CY, acc)
    acc = gram_sums(s, SLAB - 2 * CY, SLAB, acc)
    row, lane = sublanes(), lanes()
    res = jnp.zeros((8, CZ), F32)
    for b, col in enumerate(lane_sums(acc)):
        res = jnp.where(lane == NB * K + b, col, res)
    acc = [flux[i] for i in range(NP)]
    acc = flux_sums(s, ac, fx, fy, fz, 0, CY, acc, before=False)
    acc = flux_sums(s, ac, fx, fy, fz, CY, 3 * CY, acc)
    acc = flux_sums(s, ac, fx, fy, fz, SLAB - 3 * CY, SLAB - CY, acc)
    acc = flux_sums(s, ac, fx, fy, fz, SLAB - CY, SLAB, acc, after=False)
    acc = crossing_sums(s, fx, -32, 0, acc)
    acc = crossing_sums(s, fx, SLAB - CY, SLAB - 32, acc)
    for b, col in enumerate(lane_sums(acc)):
        res = jnp.where(lane == NB * K + K + b, col, res)
    part[...] = res
    wait_all(out)


def lane_sums(acc):
    row = sublanes()
    cols = []
    for b in range(K):
        x = jnp.zeros((8, CZ), F32)
        for a in range(K):
            p = PAIRS.index((min(a, b), max(a, b)))
            x = jnp.where(row == a, jnp.sum(acc[p], axis=0, keepdims=True), x)
        cols.append(jnp.sum(x, axis=1, keepdims=True))
    return cols


def couple_kernel(scal, window, near, far, part, msg, chosen, prod):
    for n in range(NB):
        m = scal[8 + n] ^ scal[3]
        place = lax.shift_right_logical(m, 1)
        odd = (m & 1) == 1
        for t in range(WMAX):
            rows = pl.ds(t * K, K)
            chosen[pl.ds((t * NB + n) * K, K), :] = jnp.where(odd, far[place, rows, :], near[place, rows, :])
    prod[:, : WMAX * NB * K] = lax.dot_general(
        window[...], chosen[...], (((1,), (1,)), ((), ())), precision=HIGHEST, preferred_element_type=F32
    )
    lane = lax.broadcasted_iota(jnp.int32, (8, 2 * CZ), 1)
    total = jnp.zeros((8, 2 * CZ), F32)
    for t in range(WMAX):
        x = jnp.zeros((8, 2 * CZ), F32)
        for n in range(NB):
            width = scal[16 + n]
            d = jnp.where(t < width, WMAX - width + t, 0)
            v = prod[pl.ds(pl.multiple_of(d * K, K), K), :]
            lo = (t * NB + n) * K
            keep = (lane >= lo) & (lane < lo + K) & (t < width)
            x = jnp.where(keep, v, x)
        total = total + (pltpu.roll(x, 2 * CZ - t * NB * K, 1) if t else x)
    res = part[...] + total[:, :CZ]
    for i in range(msg.shape[0]):
        msg[i] = res


def factor_kernel(scale, got, total, inverse, spread, galerkin):
    m = jnp.sum(got[...], axis=0) * scale
    total[...] = m
    row, lane = sublanes(), lanes()
    e = jnp.where(lane < K, pltpu.roll(m, CZ - NB * K, 1), jnp.where(lane == row + K, 1.0, 0.0))
    e = jnp.where(lane < 2 * K, e, 0.0)
    root = jnp.ones((8, 1), F32)
    for k in range(K):
        pivot = e[k : k + 1, k : k + 1]
        factor = jnp.where(row[:, :1] > k, e[:, k : k + 1] / pivot, 0.0)
        root = jnp.where(row[:, :1] == k, 1.0 / jnp.sqrt(pivot), root)
        e = e - factor * e[k : k + 1, :]
    li = jnp.where(lane < K, pltpu.roll(e * root, CZ - K, 1), 0.0)
    inverse[...] = li
    for i, (b, a) in enumerate(PAIRS):
        spread[i] = jnp.broadcast_to(li[a : a + 1, b : b + 1], (8, CZ))
    g = jnp.dot(li[:, :K], m[:, NB * K + K : NB * K + 2 * K], precision=HIGHEST, preferred_element_type=F32)
    galerkin[...] = lax.dot_general(
        g, li[:, :K], (((1,), (1,)), ((), ())), precision=HIGHEST, preferred_element_type=F32
    )


def change_kernel(si, se, spread, out):
    c = [spread[i] for i in range(NP)]
    edge = (pl.program_id(0) == 0) | (pl.program_id(0) == SLAB // CZ - 1)

    def rows(src):
        def step(i, carry):
            stores = []
            for j in range(2):
                r = pl.multiple_of(i * 16 + j * 8, 8)
                v = [src[a, pl.ds(r, 8), :] for a in range(K)]
                for a in range(K):
                    x = c[PAIRS.index((0, a))] * v[0]
                    for b in range(1, a + 1):
                        x = x + c[PAIRS.index((b, a))] * v[b]
                    stores.append((a, r, x))
            for a, r, x in stores:
                out[a, pl.ds(r, 8), :] = x
            return carry

        lax.fori_loop(0, CZ // 16, step, 0)

    @pl.when(edge)
    def _():
        rows(se.at[0])

    @pl.when(~edge)
    def _():
        rows(si)


def finish_kernel(scal, total, near, far, out):
    y = jnp.dot(near[0, :, :K], total[:, : NB * K], precision=HIGHEST, preferred_element_type=F32)
    for n in range(NB):
        m = scal[8 + n] ^ scal[3]
        place = lax.shift_right_logical(m, 1)
        li = jnp.where((m & 1) == 1, far[place], near[place])
        out[n] = lax.dot_general(
            y[:, n * K : n * K + K], li[:, :K], (((1,), (1,)), ((), ())), precision=HIGHEST,
            preferred_element_type=F32,
        )


def params(mib=40):
    return pltpu.CompilerParams(vmem_limit_bytes=mib * 1024 * 1024)


def cost(us):
    return pl.CostEstimate(flops=0, bytes_accessed=int(us * 3.0e6), transcendentals=0)


def swap(x, bits):
    return lax.ppermute(x, "subdomai", [(i, i ^ bits) for i in range(lax.axis_size("subdomai"))])


def gathered(x):
    near = jnp.stack([x, swap(x, 2), swap(x, 4), swap(x, 6)])
    return near, swap(near, 1)


def body(start_vectors, permeability, accumulation, extents, neighbour_ids, intersection_widths):
    groups = lax.axis_size("inner")
    cells = groups * SLAB * CZ
    inner = lax.axis_index("inner")
    own = lax.axis_index("subdomai")
    sv = start_vectors.reshape(K, SLAB, CZ)
    perm = permeability.reshape(SLAB, CZ)
    acc = accumulation.reshape(SLAB, CZ)
    scal = jnp.concatenate(
        [
            extents[0],
            jnp.stack([inner * 16, own]).astype(jnp.int32),
            jnp.zeros(4, jnp.int32),
            neighbour_ids[0],
            jnp.zeros(2, jnp.int32),
            intersection_widths[0],
            jnp.zeros(10, jnp.int32),
        ]
    )
    down, up = pl.pallas_call(
        pack_kernel,
        out_shape=(shape(PACK, CZ),) * 2,
        in_specs=[ANY] * 3,
        out_specs=(VMEM,) * 2,
        scratch_shapes=[pltpu.SemaphoreType.DMA((20,))],
        name="pack",
    )(sv, perm, acc)
    right = lax.ppermute(down, "inner", [(i, (i - 1) % groups) for i in range(groups)])
    left = lax.ppermute(up, "inner", [(i, (i + 1) % groups) for i in range(groups)])
    field, plain = pltpu.VMEM((K, RT, CZ), F32), pltpu.VMEM((RT, CZ), F32)
    scratch = [field] * 3 + [plain] * 6
    turning = [pltpu.VMEM((K, CZ, CZ), F32), pltpu.VMEM((CZ, CZ), F32)]
    si, ve, gram, flux, first, window = pl.pallas_call(
        interior_kernel,
        out_shape=(shape(K, INSIDE, CZ), shape(2, K, CZ, CZ))
        + (shape(NP, 8, CZ),) * 2
        + (shape(WMAX * K, INSIDE),) * 2,
        in_specs=[SMEM, ANY, ANY, ANY],
        out_specs=(ANY,) * 2 + (VMEM,) * 4,
        scratch_shapes=scratch + turning + [pltpu.SemaphoreType.DMA((3,))],
        compiler_params=params(),
        cost_estimate=cost(10),
        name="interior",
    )(scal, sv, perm, acc)
    se, first, window, part = pl.pallas_call(
        edge_kernel,
        out_shape=(shape(2, K, CZ, CZ),) + (shape(WMAX * K, SLAB),) * 2 + (shape(8, CZ),),
        in_specs=[SMEM] + [ANY] * 7 + [VMEM] * 4,
        out_specs=(ANY,) + (VMEM,) * 3,
        scratch_shapes=scratch
        + [pltpu.VMEM((WMAX * K, CZ), F32)] * 2
        + turning
        + [pltpu.SemaphoreType.DMA((30,))],
        compiler_params=params(),
        cost_estimate=cost(3),
        name="edge",
    )(scal, left, right, sv, perm, acc, si, ve, gram, flux, first, window)
    near, far = gathered(first)
    msg = pl.pallas_call(
        couple_kernel,
        out_shape=shape(groups, 8, CZ),
        in_specs=[SMEM] + [VMEM] * 4,
        out_specs=VMEM,
        scratch_shapes=[pltpu.VMEM((WMAX * NB * K, SLAB), F32), pltpu.VMEM((WMAX * K, 2 * CZ), F32)],
        compiler_params=params(),
        cost_estimate=cost(1),
        name="couple",
    )(scal, window, near, far, part)
    got = lax.all_to_all(msg, "inner", 0, 0)
    total, inverse, spread, galerkin = pl.pallas_call(
        functools.partial(factor_kernel, 1.0 / cells),
        out_shape=(shape(8, CZ), shape(8, CZ), shape(NP, 8, CZ), shape(K, K)),
        in_specs=[VMEM],
        out_specs=(VMEM,) * 4,
        compiler_params=params(),
        cost_estimate=cost(1),
        name="factor",
    )(got)
    lnear, lfar = gathered(inverse)
    basis = pl.pallas_call(
        change_kernel,
        out_shape=shape(K, SLAB, CZ),
        grid=(SLAB // CZ,),
        in_specs=[
            pl.BlockSpec((K, CZ, CZ), lambda i: (0, jnp.clip(i - 1, 0, INSIDE // CZ - 1), 0)),
            pl.BlockSpec((1, K, CZ, CZ), lambda i: (jnp.where(i > 0, 1, 0), 0, 0, 0)),
            VMEM,
        ],
        out_specs=pl.BlockSpec((K, CZ, CZ), lambda i: (0, i, 0)),
        compiler_params=params(),
        cost_estimate=cost(4),
        name="change",
    )(si, se, spread)
    coupling = pl.pallas_call(
        finish_kernel,
        out_shape=shape(NB, K, K),
        in_specs=[SMEM] + [VMEM] * 3,
        out_specs=VMEM,
        compiler_params=params(),
        cost_estimate=cost(1),
        name="finish",
    )(scal, total, lnear, lfar)
    return basis.reshape(start_vectors.shape), galerkin[None], coupling[None]


def solution(mesh):
    return jax.shard_map(
        body,
        mesh=mesh,
        in_specs=(
            P(None, ("subdomai", "inner"), None, None),
            P(("subdomai", "inner"), None, None),
            P(("subdomai", "inner"), None, None),
            P("subdomai", None),
            P("subdomai", None),
            P("subdomai", None),
        ),
        out_specs=(
            P(None, ("subdomai", "inner"), None, None),
            P("subdomai", None, None),
            P("subdomai", None, None, None),
        ),
        check_vma=False,
    )
```

```python
import functools
import jax
import jax.numpy as jnp
from jax import lax
from jax.experimental import pallas as pl
from jax.experimental.pallas import tpu as pltpu
from jax.sharding import PartitionSpec as P

F32 = jnp.float32
K = 8
NB = 6
SUBDOMAINS = 8
WMAX = 4
CY = 64
CZ = 128
OMEGA = 0.6
SLAB = 16 * CY
HALO = 160
HALO_ACC = 96
OFF = HALO + 8
RT = SLAB + 2 * OFF
PACK = K * HALO + HALO + HALO_ACC
PAIRS = [(a, b) for b in range(K) for a in range(b + 1)]
NP = len(PAIRS)
HIGHEST = lax.Precision.HIGHEST
VMEM = pl.BlockSpec(memory_space=pltpu.VMEM)
SMEM = pl.BlockSpec(memory_space=pltpu.SMEM)
HBM = pl.BlockSpec(memory_space=pltpu.HBM)
ANY = pl.BlockSpec(memory_space=pl.ANY)


def shape(*dims):
    return jax.ShapeDtypeStruct(dims, F32)


def rows_loop(lo, hi, step, init=(), tiles=4):
    def one(i, carry):
        stores = []
        for j in range(tiles):
            more, carry = step(pl.multiple_of(lo + OFF + (i * tiles + j) * 8, 8), carry)
            stores += more
        for ref, place, value in stores:
            ref[place] = value
        return carry

    assert (hi - lo) % (8 * tiles) == 0
    return lax.fori_loop(0, (hi - lo) // (8 * tiles), one, init)


def tile_at(row):
    return (pl.ds(row, 8), slice(None))


def field_at(a, row):
    return (a, pl.ds(row, 8), slice(None))


def lanes():
    return lax.broadcasted_iota(jnp.int32, (8, CZ), 1)


def sublanes():
    return lax.broadcasted_iota(jnp.int32, (8, CZ), 0)


def at(ref, row):
    return ref[pl.ds(row, 8), :]


def fat(ref, a, row):
    return ref[a, pl.ds(row, 8), :]


def layer_of(row):
    return lax.shift_right_arithmetic(row + (192 - OFF), 6) - 3


def active(scal, row, more=0):
    x = scal[2] + layer_of(row) + more
    return jnp.where((x >= 0) & (x < scal[0]), 1.0, 0.0).astype(F32)


def faces(scal, kp, fx, fy, fz, lo, hi, tiles=8):
    mz = jnp.where(lanes() < scal[1], 2.0, 0.0).astype(F32)
    mzz = jnp.where(lanes() < scal[1] - 1, 2.0, 0.0).astype(F32)
    sub = sublanes()

    def step(r, carry):
        here = active(scal, r)
        there = active(scal, r, 1)
        k = at(kp, r)
        kx = at(kp, r + CY)
        ky = at(kp, r + 1)
        kz = pltpu.roll(k, CZ - 1, 1)
        inside = jnp.where(((r + (192 - OFF)) & (CY - 1)) == CY - 8, 0.0, 1.0).astype(F32)
        my = jnp.where(sub == 7, inside, 1.0)
        stores = [
            (fx, tile_at(r), (mz * (here * there)) * k * kx / (k + kx)),
            (fy, tile_at(r), (mz * here) * my * k * ky / (k + ky)),
            (fz, tile_at(r), (mzz * here) * k * kz / (k + kz)),
        ]
        return stores, carry

    rows_loop(lo, hi, step, tiles=tiles)


def weights(ac, fx, fy, fz, w, lo, hi, tiles=8):
    def step(r, carry):
        z = at(fz, r)
        diagonal = (
            (at(ac, r) + at(fx, r))
            + (at(fx, r - CY) + at(fy, r))
            + (at(fy, r - 1) + z)
            + pltpu.roll(z, 1, 1)
        )
        return [(w, tile_at(r), OMEGA / diagonal)], carry

    rows_loop(lo, hi, step, tiles=tiles)


def smooth(scal, src, dst, fx, fy, fz, w, lo, hi, masked, tiles=16, back=0):
    mz = jnp.where(lanes() < scal[1], 1.0 - OMEGA, 0.0).astype(F32)

    def step(r, carry):
        wt = at(w, r)
        z = at(fz, r)
        xp = wt * at(fx, r)
        xm = wt * at(fx, r - CY)
        yp = wt * at(fy, r)
        ym = wt * at(fy, r - 1)
        zp = wt * z
        zm = wt * pltpu.roll(z, 1, 1)
        centre = mz * active(scal, r) if masked else 1.0 - OMEGA
        stores = []
        for a in range(K):
            v = fat(src, a, r)
            new = (
                (centre * v + xp * fat(src, a, r + CY))
                + (xm * fat(src, a, r - CY) + yp * fat(src, a, r + 1))
                + (ym * fat(src, a, r - 1) + zp * pltpu.roll(v, CZ - 1, 1))
                + zm * pltpu.roll(v, 1, 1)
            )
            stores.append((dst, field_at(a, r - back), new))
        return stores, carry

    rows_loop(lo, hi, step, tiles=tiles)


def gram_sums(s, lo, hi, acc, back=0):
    def step(r, acc):
        v = [fat(s, a, r - back) for a in range(K)]
        return [], tuple(t + v[a] * v[b] for t, (a, b) in zip(acc, PAIRS))

    return rows_loop(lo, hi, step, tuple(acc), tiles=4)


def flux_sums(s, ac, fx, fy, fz, lo, hi, acc, before=True, after=True, back=0):
    def step(r, acc):
        out = list(acc)
        z = at(fz, r)
        xp = at(fx, r)
        xm = at(fx, r - CY)
        yp = at(fy, r)
        ym = at(fy, r - 1)
        d = at(ac, r)
        q = r - back
        v = [fat(s, a, q) for a in range(K)]
        g = [c - pltpu.roll(c, CZ - 1, 1) for c in v]
        for b in range(K):
            c = v[b]
            image = d * c + yp * (c - fat(s, b, q + 1)) + ym * (c - fat(s, b, q - 1))
            if after:
                image = image + xp * (c - fat(s, b, q + CY))
            if before:
                image = image + xm * (c - fat(s, b, q - CY))
            down = z * g[b]
            for a in range(b + 1):
                p = b * (b + 1) // 2 + a
                out[p] = out[p] + (v[a] * image + g[a] * down)
        return [], tuple(out)

    return rows_loop(lo, hi, step, tuple(acc), tiles=4)


def crossing_sums(s, fx, lo, hi, acc):
    def step(r, acc):
        f = at(fx, r)
        d = [fat(s, a, r) - fat(s, a, r + CY) for a in range(K)]
        e = [f * t for t in d]
        return [], tuple(t + d[a] * e[b] for t, (a, b) in zip(acc, PAIRS))

    return rows_loop(lo, hi, step, tuple(acc), tiles=1)


def turned(scal, s, kp, first, window, tile, ptile, blocks, back=0):
    start = scal[1] - WMAX

    def step(block, row, lane):
        ptile[...] = kp[pl.ds(row, CZ), :].T
        kw = ptile[pl.ds(start, WMAX), :]
        for a in range(K):
            tile[a] = s[a, pl.ds(pl.multiple_of(row - back, 8), CZ), :].T
        for a in range(K):
            u = tile[a, pl.ds(start, WMAX), :] * kw
            f = tile[a, pl.ds(0, WMAX), :]
            for t in range(WMAX):
                first[pl.ds(t * K + a, 1), pl.ds(lane, CZ)] = f[t : t + 1]
                window[pl.ds(t * K + a, 1), pl.ds(lane, CZ)] = u[t : t + 1]

    def one(block, carry):
        step(block, pl.multiple_of(OFF + block * CZ, 8), pl.multiple_of((block - blocks[0]) * CZ, CZ))
        return carry

    lax.fori_loop(blocks[0], blocks[1], one, 0)


def copy_all(pairs, sem):
    copies = [pltpu.make_async_copy(src, dst, sem.at[i]) for i, (src, dst) in enumerate(pairs)]
    for c in copies:
        c.start()
    return copies


def wait_all(copies):
    for c in copies:
        c.wait()


def pack_kernel(sv, perm, acc, down, up, sem):
    pairs = []
    for out, lo, acc_lo in ((down, 0, 0), (up, SLAB - HALO, SLAB - HALO_ACC)):
        for a in range(K):
            pairs.append((sv.at[a, pl.ds(lo, HALO)], out.at[pl.ds(a * HALO, HALO)]))
        pairs.append((perm.at[pl.ds(lo, HALO)], out.at[pl.ds(K * HALO, HALO)]))
        pairs.append((acc.at[pl.ds(acc_lo, HALO_ACC)], out.at[pl.ds((K + 1) * HALO, HALO_ACC)]))
    wait_all(copy_all(pairs, sem))


INSIDE = SLAB - 4 * CY
EDGE = 2 * CY + 32
FIRST = WMAX * K
SENT = SLAB // CZ * FIRST + 8


BACK = OFF + 2 * CY


def interior_kernel(
    scal, sv, perm, acc, si, ve, fx, fy, fz, w, gram, first, window, v0, v1, kp, ac, tile, ptile, sem
):
    slab = pl.ds(OFF, SLAB)
    a, b, c = copy_all([(perm, kp.at[slab]), (acc, ac.at[slab]), (sv, v0.at[:, slab])], sem)
    a.wait()
    faces(scal, kp, fx, fy, fz, 0, SLAB - CY)
    b.wait()
    weights(ac, fx, fy, fz, w, CY, SLAB - CY)
    c.wait()
    smooth(scal, v0, v1, fx, fy, fz, w, CY, SLAB - CY, True)
    out = copy_all(
        [
            (v0.at[:, pl.ds(OFF, CZ)], ve.at[0]),
            (v0.at[:, pl.ds(OFF + SLAB - CZ, CZ)], ve.at[1]),
            (v1.at[:, pl.ds(OFF + CY, CZ)], ve.at[2]),
            (v1.at[:, pl.ds(OFF + SLAB - CY - CZ, CZ)], ve.at[3]),
        ],
        sem,
    )
    smooth(scal, v1, si, fx, fy, fz, w, 2 * CY, SLAB - 2 * CY, False, back=BACK)
    zero = [jnp.zeros((8, CZ), F32)] * NP
    for i, t in enumerate(gram_sums(si, 2 * CY, SLAB - 2 * CY, zero, back=BACK)):
        gram[i] = t
    turned(scal, si, kp, first, window, tile, ptile, (1, 7), back=BACK)
    wait_all(out)


def edge_kernel(
    scal, left, right, perm, acc, ve, fxi, fyi, fzi, wi, gram, firsti, windowi,
    se, sent, window, fx, fy, fz, v0, v1, s, kp, ac, w, fe, we, tile, ptile, sem,
):
    pairs = []
    own = SLAB - CZ
    for src, lo, acc_lo, near in ((left, -HALO, -HALO_ACC, 0), (right, SLAB, SLAB, own)):
        pairs.append((src.at[pl.ds(K * HALO, HALO)], kp.at[pl.ds(OFF + lo, HALO)]))
        pairs.append((src.at[pl.ds((K + 1) * HALO, HALO_ACC)], ac.at[pl.ds(OFF + acc_lo, HALO_ACC)]))
        pairs.append((perm.at[pl.ds(near, CZ)], kp.at[pl.ds(OFF + near, CZ)]))
        pairs.append((acc.at[pl.ds(near, CZ)], ac.at[pl.ds(OFF + near, CZ)]))
    early = len(pairs)
    for src, lo in ((left, -HALO), (right, SLAB)):
        for a in range(K):
            pairs.append((src.at[pl.ds(a * HALO, HALO)], v0.at[a, pl.ds(OFF + lo, HALO)]))
    for old, new in ((fxi, fx), (fyi, fy), (fzi, fz)):
        for near, count in ((0, 3 * CY), (SLAB - 4 * CY, 3 * CY)):
            rows = pl.ds(OFF + near, count)
            pairs.append((old.at[rows], new.at[rows]))
    for near in (CY, SLAB - 2 * CY):
        rows = pl.ds(OFF + near, CY)
        pairs.append((wi.at[rows], w.at[rows]))
    pairs.append((ve.at[0], v0.at[:, pl.ds(OFF, CZ)]))
    pairs.append((ve.at[1], v0.at[:, pl.ds(OFF + own, CZ)]))
    pairs.append((ve.at[2], v1.at[:, pl.ds(OFF + CY, CZ)]))
    pairs.append((ve.at[3], v1.at[:, pl.ds(OFF + SLAB - CY - CZ, CZ)]))
    copies = copy_all(pairs, sem)
    wait_all(copies[:early])
    wait_all(copies[early:])
    faces(scal, kp, fx, fy, fz, -HALO, 0, 20)
    faces(scal, kp, fx, fy, fz, SLAB - CY, SLAB + HALO_ACC, 20)
    weights(ac, fx, fy, fz, w, -HALO_ACC, CY, 20)
    weights(ac, fx, fy, fz, w, SLAB - CY, SLAB + HALO_ACC, 20)
    smooth(scal, v0, v1, fx, fy, fz, w, -HALO_ACC, CY, True, 20)
    smooth(scal, v0, v1, fx, fy, fz, w, SLAB - CY, SLAB + HALO_ACC, True, 20)
    smooth(scal, v1, s, fx, fy, fz, w, -32, 2 * CY, False, 20)
    smooth(scal, v1, s, fx, fy, fz, w, SLAB - 2 * CY, SLAB + 32, False, 20)
    out = copy_all(
        [
            (s.at[:, pl.ds(OFF - 32, EDGE)], se.at[0]),
            (s.at[:, pl.ds(OFF + own, EDGE)], se.at[1]),
        ],
        sem,
    )
    window[:, pl.ds(CZ, INSIDE)] = windowi[...]
    for i in range(INSIDE // CZ):
        sent[pl.ds((i + 1) * FIRST, FIRST), :] = firsti[:, i * CZ : (i + 1) * CZ]
    for i, lane in ((0, 0), (7, own)):
        turned(scal, s, kp, fe, we, tile, ptile, (i, i + 1))
        sent[pl.ds(i * FIRST, FIRST), :] = fe[...]
        window[:, pl.ds(lane, CZ)] = we[...]
    acc = [gram[i] for i in range(NP)]
    acc = gram_sums(s, 0, 2 * CY, acc)
    acc = gram_sums(s, SLAB - 2 * CY, SLAB, acc)
    lane = lanes()
    res = jnp.zeros((8, CZ), F32)
    for b, col in enumerate(lane_sums(acc)):
        res = jnp.where(lane == b, col, res)
    sent[pl.ds(SENT - 8, 8), :] = res
    wait_all(out)


def flux_kernel(se, si, acc, fxi, fyi, fzi, fx, fy, fz, part, s, ac, sem):
    own = SLAB - CZ
    wait_all(
        copy_all(
            [
                (se.at[0], s.at[:, pl.ds(OFF - 32, EDGE)]),
                (se.at[1], s.at[:, pl.ds(OFF + own, EDGE)]),
                (si.at[:, pl.ds(0, CZ)], s.at[:, pl.ds(OFF + CZ, CZ)]),
                (si.at[:, pl.ds(INSIDE - CZ, CZ)], s.at[:, pl.ds(OFF + own - CZ, CZ)]),
                (acc, ac.at[pl.ds(OFF, SLAB)]),
            ],
            sem,
        )
    )
    acc = [jnp.zeros((8, CZ), F32)] * NP
    acc = flux_sums(si, ac, fxi, fyi, fzi, 3 * CY, SLAB - 3 * CY, acc, back=BACK)
    acc = flux_sums(s, ac, fx, fy, fz, 0, CY, acc, before=False)
    acc = flux_sums(s, ac, fx, fy, fz, CY, 3 * CY, acc)
    acc = flux_sums(s, ac, fx, fy, fz, SLAB - 3 * CY, SLAB - CY, acc)
    acc = flux_sums(s, ac, fx, fy, fz, SLAB - CY, SLAB, acc, after=False)
    acc = crossing_sums(s, fx, -32, 0, acc)
    acc = crossing_sums(s, fx, SLAB - CY, SLAB - 32, acc)
    lane = lanes()
    res = jnp.zeros((8, CZ), F32)
    for b, col in enumerate(lane_sums(acc)):
        res = jnp.where(lane == b, col, res)
    part[...] = res


def lane_sums(acc):
    row = sublanes()
    cols = []
    for b in range(K):
        x = jnp.zeros((8, CZ), F32)
        for a in range(K):
            p = PAIRS.index((min(a, b), max(a, b)))
            x = jnp.where(row == a, jnp.sum(acc[p], axis=0, keepdims=True), x)
        cols.append(jnp.sum(x, axis=1, keepdims=True))
    return cols


GRAM = NB * K
FLUX = GRAM + K
OTHERS = FLUX + K


def couple_kernel(scal, window, near, far, part, msg, chosen, prod):
    for n in range(NB):
        m = scal[8 + n] ^ scal[3]
        place = lax.shift_right_logical(m, 1)
        odd = (m & 1) == 1
        for i in range(SLAB // CZ):
            for t in range(WMAX):
                rows = pl.ds(i * FIRST + t * K, K)
                value = jnp.where(odd, far[place, rows, :], near[place, rows, :])
                chosen[pl.ds((t * NB + n) * K, K), i * CZ : (i + 1) * CZ] = value
    prod[:, : WMAX * NB * K] = lax.dot_general(
        window[...], chosen[...], (((1,), (1,)), ((), ())), precision=HIGHEST, preferred_element_type=F32
    )
    lane = lax.broadcasted_iota(jnp.int32, (8, 2 * CZ), 1)
    total = jnp.zeros((8, 2 * CZ), F32)
    for t in range(WMAX):
        x = jnp.zeros((8, 2 * CZ), F32)
        for n in range(NB):
            width = scal[16 + n]
            d = jnp.where(t < width, WMAX - width + t, 0)
            v = prod[pl.ds(pl.multiple_of(d * K, K), K), :]
            lo = (t * NB + n) * K
            keep = (lane >= lo) & (lane < lo + K) & (t < width)
            x = jnp.where(keep, v, x)
        total = total + (pltpu.roll(x, 2 * CZ - t * NB * K, 1) if t else x)
    lane = lanes()
    res = jnp.where(lane < GRAM, total[:, :CZ], 0.0)
    res = res + pltpu.roll(part[...], FLUX, 1)
    for m in range(SUBDOMAINS):
        g = (far if m & 1 else near)[m // 2, pl.ds(SENT - 8, 8), :]
        res = res + pltpu.roll(g, OTHERS + (m - 1) * K if m else GRAM, 1)
    for i in range(msg.shape[0]):
        msg[i] = res


def eliminate(grams):
    row, lane = sublanes(), lanes()
    column = row[:, :1]
    es = []
    for g in grams:
        e = jnp.where(lane < K, g, jnp.where(lane == row + K, 1.0, 0.0))
        es.append(jnp.where(lane < 2 * K, e, 0.0))
    roots = [jnp.ones((8, 1), F32)] * len(es)
    for k in range(K):
        for m, e in enumerate(es):
            pivot = e[k : k + 1, k : k + 1]
            factor = jnp.where(column > k, e[:, k : k + 1] / pivot, 0.0)
            roots[m] = jnp.where(column == k, 1.0 / jnp.sqrt(pivot), roots[m])
            es[m] = e - factor * e[k : k + 1, :]
    return [jnp.where(lane < K, pltpu.roll(e * root, CZ - K, 1), 0.0) for e, root in zip(es, roots)]


def finish_kernel(scale, scal, got, si, se, basis, galerkin, coupling, inverse, out, sem):
    total = jnp.sum(got[...], axis=0) * scale
    (li,) = eliminate([pltpu.roll(total, CZ - GRAM, 1)])
    inverse[0] = li
    c = {(b, a): jnp.broadcast_to(li[a : a + 1, b : b + 1], (8, CZ)) for b, a in PAIRS}
    copies = []
    for i in range(SLAB // CZ):
        if i == 0:
            src = se.at[0, :, pl.ds(32, CZ)]
        elif i == SLAB // CZ - 1:
            src = se.at[1, :, pl.ds(0, CZ)]
        else:
            src = si.at[:, pl.ds((i - 1) * CZ, CZ)]

        def step(j, carry, src=src, i=i):
            stores = []
            for t in range(4):
                r = pl.multiple_of(j * 32 + t * 8, 8)
                v = [src[a, pl.ds(r, 8), :] for a in range(K)]
                for a in range(K):
                    x = c[0, a] * v[0]
                    for b in range(1, a + 1):
                        x = x + c[b, a] * v[b]
                    stores.append((a, r, x))
            for a, r, x in stores:
                out[i, a, pl.ds(r, 8), :] = x
            return carry

        lax.fori_loop(0, CZ // 32, step, 0)
        copies.append(pltpu.make_async_copy(out.at[i], basis.at[:, pl.ds(i * CZ, CZ)], sem.at[i]))
        copies[-1].start()
    others = eliminate([pltpu.roll(total, CZ - OTHERS - m * K, 1) for m in range(SUBDOMAINS - 1)])
    for m, other in enumerate(others):
        inverse[m + 1] = other
    y = jnp.dot(li[:, :K], total[:, :OTHERS], precision=HIGHEST, preferred_element_type=F32)
    transposed = (((1,), (1,)), ((), ()))
    galerkin[...] = lax.dot_general(
        y[:, FLUX:OTHERS], li[:, :K], transposed, precision=HIGHEST, preferred_element_type=F32
    )
    for n in range(NB):
        other = inverse[scal[8 + n] ^ scal[3]]
        coupling[n] = lax.dot_general(
            y[:, n * K : n * K + K], other[:, :K], transposed, precision=HIGHEST, preferred_element_type=F32
        )
    wait_all(copies)


def params(mib=40):
    return pltpu.CompilerParams(vmem_limit_bytes=mib * 1024 * 1024)


def cost(us):
    return pl.CostEstimate(flops=0, bytes_accessed=int(us * 3.0e6), transcendentals=0)


def swap(x, bits):
    return lax.ppermute(x, "subdomai", [(i, i ^ bits) for i in range(lax.axis_size("subdomai"))])


def body(start_vectors, permeability, accumulation, extents, neighbour_ids, intersection_widths):
    groups = lax.axis_size("inner")
    cells = groups * SLAB * CZ
    inner = lax.axis_index("inner")
    own = lax.axis_index("subdomai")
    sv = start_vectors.reshape(K, SLAB, CZ)
    perm = permeability.reshape(SLAB, CZ)
    acc = accumulation.reshape(SLAB, CZ)
    scal = jnp.concatenate(
        [
            extents[0],
            jnp.stack([inner * 16, own]).astype(jnp.int32),
            jnp.zeros(4, jnp.int32),
            neighbour_ids[0],
            jnp.zeros(2, jnp.int32),
            intersection_widths[0],
            jnp.zeros(10, jnp.int32),
        ]
    )
    down, up = pl.pallas_call(
        pack_kernel,
        out_shape=(shape(PACK, CZ),) * 2,
        in_specs=[HBM] * 3,
        out_specs=(VMEM,) * 2,
        scratch_shapes=[pltpu.SemaphoreType.DMA((20,))],
        compiler_params=params(60),
        name="pack",
    )(sv, perm, acc)
    right = lax.ppermute(down, "inner", [(i, (i - 1) % groups) for i in range(groups)])
    left = lax.ppermute(up, "inner", [(i, (i + 1) % groups) for i in range(groups)])
    field, plain = pltpu.VMEM((K, RT, CZ), F32), pltpu.VMEM((RT, CZ), F32)
    turning = [pltpu.VMEM((K, CZ, CZ), F32), pltpu.VMEM((CZ, CZ), F32)]
    turn = shape(FIRST, INSIDE)
    si, ve, fx, fy, fz, w, gram, first, window = pl.pallas_call(
        interior_kernel,
        out_shape=(shape(K, INSIDE, CZ), shape(4, K, CZ, CZ))
        + (shape(RT, CZ),) * 4
        + (shape(NP, 8, CZ),)
        + (turn,) * 2,
        in_specs=[SMEM, HBM, HBM, HBM],
        out_specs=(VMEM,) * 9,
        scratch_shapes=[field] * 2 + [plain] * 2 + turning + [pltpu.SemaphoreType.DMA((4,))],
        compiler_params=params(40),
        cost_estimate=cost(13),
        name="interior",
    )(scal, sv, perm, acc)
    se, sent, window, fxe, fye, fze = pl.pallas_call(
        edge_kernel,
        out_shape=(shape(2, K, EDGE, CZ), shape(SENT, CZ), shape(FIRST, SLAB)) + (shape(RT, CZ),) * 3,
        in_specs=[SMEM] + [VMEM] * 2 + [HBM] * 2 + [VMEM] * 8,
        out_specs=(VMEM,) * 6,
        scratch_shapes=[field] * 3
        + [plain] * 3
        + [pltpu.VMEM((FIRST, CZ), F32)] * 2
        + turning
        + [pltpu.SemaphoreType.DMA((48,))],
        compiler_params=params(24),
        cost_estimate=cost(6),
        name="edge",
    )(scal, left, right, perm, acc, ve, fx, fy, fz, w, gram, first, window)
    moved = [swap(sent, bits) for bits in (2, 4, 6)]
    part = pl.pallas_call(
        flux_kernel,
        out_shape=shape(8, CZ),
        in_specs=[VMEM] * 2 + [HBM] + [VMEM] * 6,
        out_specs=VMEM,
        scratch_shapes=[field, plain, pltpu.SemaphoreType.DMA((5,))],
        compiler_params=params(10),
        cost_estimate=cost(6),
        name="flux",
    )(se, si, acc, fx, fy, fz, fxe, fye, fze)
    moved, part = lax.optimization_barrier((moved, part))
    near = jnp.stack([sent] + moved)
    far = swap(near, 1)
    msg = pl.pallas_call(
        couple_kernel,
        out_shape=shape(groups, 8, CZ),
        in_specs=[SMEM] + [VMEM] * 4,
        out_specs=VMEM,
        scratch_shapes=[pltpu.VMEM((WMAX * NB * K, SLAB), F32), pltpu.VMEM((FIRST, 2 * CZ), F32)],
        compiler_params=params(8),
        cost_estimate=cost(1),
        name="couple",
    )(scal, window, near, far, part)
    got = lax.all_to_all(msg, "inner", 0, 0)
    basis, galerkin, coupling = pl.pallas_call(
        functools.partial(finish_kernel, 1.0 / cells),
        out_shape=(shape(K, SLAB, CZ), shape(K, K), shape(NB, K, K)),
        in_specs=[SMEM] + [VMEM] * 3,
        out_specs=(HBM, VMEM, VMEM),
        scratch_shapes=[
            pltpu.VMEM((SUBDOMAINS, 8, CZ), F32),
            pltpu.VMEM((SLAB // CZ, K, CZ, CZ), F32),
            pltpu.SemaphoreType.DMA((SLAB // CZ,)),
        ],
        compiler_params=params(8),
        cost_estimate=cost(5),
        name="finish",
    )(scal, got, si, se)
    return basis.reshape(start_vectors.shape), galerkin[None], coupling[None]


def solution(mesh):
    return jax.shard_map(
        body,
        mesh=mesh,
        in_specs=(
            P(None, ("subdomai", "inner"), None, None),
            P(("subdomai", "inner"), None, None),
            P(("subdomai", "inner"), None, None),
            P("subdomai", None),
            P("subdomai", None),
            P("subdomai", None),
        ),
        out_specs=(
            P(None, ("subdomai", "inner"), None, None),
            P("subdomai", None, None),
            P("subdomai", None, None, None),
        ),
        check_vma=False,
    )
```

```python
import functools
import jax
import jax.numpy as jnp
from jax import lax
from jax.experimental import pallas as pl
from jax.experimental.pallas import tpu as pltpu
from jax.sharding import PartitionSpec as P

F32 = jnp.float32
K = 8
NB = 6
SUBDOMAINS = 8
WMAX = 4
CY = 64
CZ = 128
OMEGA = 0.6
SLAB = 16 * CY
HALO = 160
HALO_ACC = 96
OFF = HALO + 8
RT = SLAB + 2 * OFF
PACK = K * HALO + HALO + HALO_ACC
PAIRS = [(a, b) for b in range(K) for a in range(b + 1)]
NP = len(PAIRS)
BY_MATRIX = 4
HIGHEST = lax.Precision.HIGHEST
VMEM = pl.BlockSpec(memory_space=pltpu.VMEM)
SMEM = pl.BlockSpec(memory_space=pltpu.SMEM)
HBM = pl.BlockSpec(memory_space=pltpu.HBM)
ANY = pl.BlockSpec(memory_space=pl.ANY)


def shape(*dims):
    return jax.ShapeDtypeStruct(dims, F32)


def rows_loop(lo, hi, step, init=(), tiles=4):
    def one(i, carry):
        stores = []
        for j in range(tiles):
            more, carry = step(pl.multiple_of(lo + OFF + (i * tiles + j) * 8, 8), carry)
            stores += more
        for ref, place, value in stores:
            ref[place] = value
        return carry

    assert (hi - lo) % (8 * tiles) == 0
    return lax.fori_loop(0, (hi - lo) // (8 * tiles), one, init)


def tile_at(row):
    return (pl.ds(row, 8), slice(None))


def field_at(a, row):
    return (a, pl.ds(row, 8), slice(None))


def lanes():
    return lax.broadcasted_iota(jnp.int32, (8, CZ), 1)


def sublanes():
    return lax.broadcasted_iota(jnp.int32, (8, CZ), 0)


def at(ref, row):
    return ref[pl.ds(row, 8), :]


def fat(ref, a, row):
    return ref[a, pl.ds(row, 8), :]


def layer_of(row):
    return lax.shift_right_arithmetic(row + (192 - OFF), 6) - 3


def active(scal, row, more=0):
    x = scal[2] + layer_of(row) + more
    return jnp.where((x >= 0) & (x < scal[0]), 1.0, 0.0).astype(F32)


def faces(scal, kp, fx, fy, fz, lo, hi, tiles=8):
    mz = jnp.where(lanes() < scal[1], 2.0, 0.0).astype(F32)
    mzz = jnp.where(lanes() < scal[1] - 1, 2.0, 0.0).astype(F32)
    sub = sublanes()

    def step(r, carry):
        here = active(scal, r)
        there = active(scal, r, 1)
        k = at(kp, r)
        kx = at(kp, r + CY)
        ky = at(kp, r + 1)
        kz = pltpu.roll(k, CZ - 1, 1)
        inside = jnp.where(((r + (192 - OFF)) & (CY - 1)) == CY - 8, 0.0, 1.0).astype(F32)
        my = jnp.where(sub == 7, inside, 1.0)
        stores = [
            (fx, tile_at(r), (mz * (here * there)) * k * kx / (k + kx)),
            (fy, tile_at(r), (mz * here) * my * k * ky / (k + ky)),
            (fz, tile_at(r), (mzz * here) * k * kz / (k + kz)),
        ]
        return stores, carry

    rows_loop(lo, hi, step, tiles=tiles)


def weights(ac, fx, fy, fz, w, lo, hi, tiles=8):
    def step(r, carry):
        z = at(fz, r)
        diagonal = (
            (at(ac, r) + at(fx, r))
            + (at(fx, r - CY) + at(fy, r))
            + (at(fy, r - 1) + z)
            + pltpu.roll(z, 1, 1)
        )
        return [(w, tile_at(r), OMEGA / diagonal)], carry

    rows_loop(lo, hi, step, tiles=tiles)


def shifter():
    row = lax.broadcasted_iota(jnp.int32, (2 * CZ, 2 * CZ), 0) & (CZ - 1)
    col = lax.broadcasted_iota(jnp.int32, (2 * CZ, 2 * CZ), 1)
    source = jnp.where(col < CZ, col + 1, col + CZ - 1) & (CZ - 1)
    return jnp.where(row == source, 1.0, 0.0).astype(F32).astype(jnp.bfloat16)


def smooth(scal, src, dst, fx, fy, fz, w, lo, hi, masked, tiles=16, back=0, by_matrix=BY_MATRIX):
    mz = jnp.where(lanes() < scal[1], 1.0 - OMEGA, 0.0).astype(F32)
    shift = shifter()

    def step(i, carry):
        top = pl.multiple_of(lo + OFF + i * tiles * 8, 8)
        moved = {}
        for a in range(by_matrix):
            v = src[a, pl.ds(top, tiles * 8), :]
            high = v.astype(jnp.bfloat16)
            low = (v - high.astype(F32)).astype(jnp.bfloat16)
            moved[a] = jnp.dot(jnp.concatenate([high, low], axis=1), shift, preferred_element_type=F32)
        stores = []
        for j in range(tiles):
            r = pl.multiple_of(top + j * 8, 8)
            wt = at(w, r)
            z = at(fz, r)
            xp = wt * at(fx, r)
            xm = wt * at(fx, r - CY)
            yp = wt * at(fy, r)
            ym = wt * at(fy, r - 1)
            zp = wt * z
            zm = wt * pltpu.roll(z, 1, 1)
            centre = mz * active(scal, r) if masked else 1.0 - OMEGA
            for a in range(K):
                v = fat(src, a, r)
                if a in moved:
                    after = moved[a][j * 8 : j * 8 + 8, :CZ]
                    before = moved[a][j * 8 : j * 8 + 8, CZ:]
                else:
                    after = pltpu.roll(v, CZ - 1, 1)
                    before = pltpu.roll(v, 1, 1)
                new = (
                    (centre * v + xp * fat(src, a, r + CY))
                    + (xm * fat(src, a, r - CY) + yp * fat(src, a, r + 1))
                    + (ym * fat(src, a, r - 1) + zp * after)
                    + zm * before
                )
                stores.append((dst, field_at(a, r - back), new))
        for ref, place, value in stores:
            ref[place] = value
        return carry

    assert (hi - lo) % (8 * tiles) == 0
    lax.fori_loop(0, (hi - lo) // (8 * tiles), step, 0)


def gram_sums(s, lo, hi, acc, back=0):
    def step(r, acc):
        v = [fat(s, a, r - back) for a in range(K)]
        return [], tuple(t + v[a] * v[b] for t, (a, b) in zip(acc, PAIRS))

    return rows_loop(lo, hi, step, tuple(acc), tiles=4)


def flux_sums(s, ac, fx, fy, fz, lo, hi, acc, before=True, after=True, back=0):
    def step(r, acc):
        out = list(acc)
        z = at(fz, r)
        xp = at(fx, r)
        xm = at(fx, r - CY)
        yp = at(fy, r)
        ym = at(fy, r - 1)
        d = at(ac, r)
        q = r - back
        v = [fat(s, a, q) for a in range(K)]
        g = [c - pltpu.roll(c, CZ - 1, 1) for c in v]
        for b in range(K):
            c = v[b]
            image = d * c + yp * (c - fat(s, b, q + 1)) + ym * (c - fat(s, b, q - 1))
            if after:
                image = image + xp * (c - fat(s, b, q + CY))
            if before:
                image = image + xm * (c - fat(s, b, q - CY))
            down = z * g[b]
            for a in range(b + 1):
                p = b * (b + 1) // 2 + a
                out[p] = out[p] + (v[a] * image + g[a] * down)
        return [], tuple(out)

    return rows_loop(lo, hi, step, tuple(acc), tiles=4)


def crossing_sums(s, fx, lo, hi, acc):
    def step(r, acc):
        f = at(fx, r)
        d = [fat(s, a, r) - fat(s, a, r + CY) for a in range(K)]
        e = [f * t for t in d]
        return [], tuple(t + d[a] * e[b] for t, (a, b) in zip(acc, PAIRS))

    return rows_loop(lo, hi, step, tuple(acc), tiles=1)


def turned(scal, s, kp, first, window, tile, ptile, blocks, back=0):
    start = scal[1] - WMAX

    def step(block, row, lane):
        ptile[...] = kp[pl.ds(row, CZ), :].T
        kw = ptile[pl.ds(start, WMAX), :]
        for a in range(K):
            tile[a] = s[a, pl.ds(pl.multiple_of(row - back, 8), CZ), :].T
        for a in range(K):
            u = tile[a, pl.ds(start, WMAX), :] * kw
            f = tile[a, pl.ds(0, WMAX), :]
            for t in range(WMAX):
                first[pl.ds(t * K + a, 1), pl.ds(lane, CZ)] = f[t : t + 1]
                window[pl.ds(t * K + a, 1), pl.ds(lane, CZ)] = u[t : t + 1]

    def one(block, carry):
        step(block, pl.multiple_of(OFF + block * CZ, 8), pl.multiple_of((block - blocks[0]) * CZ, CZ))
        return carry

    lax.fori_loop(blocks[0], blocks[1], one, 0)


def copy_all(pairs, sem):
    copies = [pltpu.make_async_copy(src, dst, sem.at[i]) for i, (src, dst) in enumerate(pairs)]
    for c in copies:
        c.start()
    return copies


def wait_all(copies):
    for c in copies:
        c.wait()


def pack_kernel(sv, perm, acc, down, up, sem):
    pairs = []
    for out, lo, acc_lo in ((down, 0, 0), (up, SLAB - HALO, SLAB - HALO_ACC)):
        pairs.append((sv.at[:, pl.ds(lo, HALO)], out.at[pl.ds(0, K * HALO)].reshape(K, HALO, CZ)))
        pairs.append((perm.at[pl.ds(lo, HALO)], out.at[pl.ds(K * HALO, HALO)]))
        pairs.append((acc.at[pl.ds(acc_lo, HALO_ACC)], out.at[pl.ds((K + 1) * HALO, HALO_ACC)]))
    wait_all(copy_all(pairs, sem))


INSIDE = SLAB - 4 * CY
EDGE = 2 * CY + 32
FIRST = WMAX * K
SENT = SLAB // CZ * FIRST + 8


BACK = OFF + 2 * CY
OWN = SLAB - CZ
EDGE_BACK = (OFF - 32, OFF + OWN)


def copy_rows(moves, count, group):
    def one(i, carry):
        values = []
        for j in range(group):
            for dst, at_dst, src, at_src in moves:
                rows = [pl.ds(pl.multiple_of(r + (i * group + j) * 8, 8), 8) for r in (at_dst, at_src)]
                if len(dst.shape) == 2:
                    values.append((dst, (rows[0], slice(None)), src[rows[1], :]))
                else:
                    for a in range(K):
                        values.append((dst, (a, rows[0], slice(None)), src[a, rows[1], :]))
        for dst, place, value in values:
            dst[place] = value
        return carry

    assert count % (8 * group) == 0
    lax.fori_loop(0, count // (8 * group), one, 0)


def interior_kernel(
    scal, sv, perm, acc, si, ve, kp, ac, fx, fy, fz, w, gram, flux, first, window, v0, v1, tile, ptile, sem
):
    slab = pl.ds(OFF, SLAB)
    a, b, c = copy_all([(perm, kp.at[slab]), (acc, ac.at[slab]), (sv, v0.at[:, slab])], sem)
    a.wait()
    faces(scal, kp, fx, fy, fz, 0, SLAB - CY, 20)
    b.wait()
    weights(ac, fx, fy, fz, w, CY, SLAB - CY, 16)
    c.wait()
    smooth(scal, v0, v1, fx, fy, fz, w, CY, SLAB - CY, True)
    out = copy_all(
        [
            (v0.at[:, pl.ds(OFF, CZ)], ve.at[0]),
            (v0.at[:, pl.ds(OFF + OWN, CZ)], ve.at[1]),
            (v1.at[:, pl.ds(OFF + CY, CZ)], ve.at[2]),
            (v1.at[:, pl.ds(OFF + SLAB - CY - CZ, CZ)], ve.at[3]),
        ],
        sem,
    )
    smooth(scal, v1, si, fx, fy, fz, w, 2 * CY, SLAB - 2 * CY, False, back=BACK)
    zero = [jnp.zeros((8, CZ), F32)] * NP
    for i, t in enumerate(gram_sums(si, 2 * CY, SLAB - 2 * CY, zero, back=BACK)):
        gram[i] = t
    for i, t in enumerate(flux_sums(si, ac, fx, fy, fz, 3 * CY, SLAB - 3 * CY, zero, back=BACK)):
        flux[i] = t
    turned(scal, si, kp, first, window, tile, ptile, (1, 7), back=BACK)
    wait_all(out)


def edge_kernel(
    scal, left, right, ve, kpi, aci, fxi, fyi, fzi, wi, gram, firsti, windowi,
    se, sent, window, fx, fy, fz, v0, v1, kp, ac, w, fe, we, tile, ptile,
):
    ends = ((left, -HALO, -HALO_ACC, 0), (right, SLAB, SLAB, OWN))
    moves = [(kp, OFF + lo, src, K * HALO) for src, lo, _, _ in ends]
    copy_rows(moves, HALO, 20)
    moves = [(ac, OFF + lo, src, (K + 1) * HALO) for src, _, lo, _ in ends]
    copy_rows(moves, HALO_ACC, 12)
    copy_rows([(new, OFF + n, old, OFF + n) for new, old in ((kp, kpi), (ac, aci)) for n in (0, OWN)], CZ, 16)
    both = (0, SLAB - 4 * CY)
    copy_rows([(new, OFF + n, old, OFF + n) for new, old in ((fx, fxi), (fy, fyi), (fz, fzi)) for n in both], 3 * CY, 8)
    copy_rows([(w, OFF + n, wi, OFF + n) for n in (CY, SLAB - 2 * CY)], CY, 8)
    faces(scal, kp, fx, fy, fz, -HALO, 0, 20)
    faces(scal, kp, fx, fy, fz, SLAB - CY, SLAB + HALO_ACC, 20)
    weights(ac, fx, fy, fz, w, -HALO_ACC, CY, 20)
    weights(ac, fx, fy, fz, w, SLAB - CY, SLAB + HALO_ACC, 20)
    for src, lo, _, _ in ends:
        for a in range(K):
            copy_rows([(v0.at[a], OFF + lo, src, a * HALO)], HALO, 20)
    for i, near in enumerate((0, OWN)):
        copy_rows([(v0, OFF + near, ve.at[i], 0)], CZ, 8)
    for i, near in enumerate((CY, SLAB - CY - CZ)):
        copy_rows([(v1, OFF + near, ve.at[2 + i], 0)], CZ, 8)
    smooth(scal, v0, v1, fx, fy, fz, w, -HALO_ACC, CY, True, 20)
    smooth(scal, v0, v1, fx, fy, fz, w, SLAB - CY, SLAB + HALO_ACC, True, 20)
    smooth(scal, v1, se.at[0], fx, fy, fz, w, -32, 2 * CY, False, 20, EDGE_BACK[0])
    smooth(scal, v1, se.at[1], fx, fy, fz, w, SLAB - 2 * CY, SLAB + 32, False, 20, EDGE_BACK[1])
    window[:, pl.ds(CZ, INSIDE)] = windowi[...]
    for i in range(INSIDE // CZ):
        sent[pl.ds((i + 1) * FIRST, FIRST), :] = firsti[:, i * CZ : (i + 1) * CZ]
    for i, lane, end in ((0, 0, 0), (7, OWN, 1)):
        turned(scal, se.at[end], kp, fe, we, tile, ptile, (i, i + 1), EDGE_BACK[end])
        sent[pl.ds(i * FIRST, FIRST), :] = fe[...]
        window[:, pl.ds(lane, CZ)] = we[...]
    acc = [gram[i] for i in range(NP)]
    acc = gram_sums(se.at[0], 0, 2 * CY, acc, EDGE_BACK[0])
    acc = gram_sums(se.at[1], SLAB - 2 * CY, SLAB, acc, EDGE_BACK[1])
    lane = lanes()
    res = jnp.zeros((8, CZ), F32)
    for b, col in enumerate(lane_sums(acc)):
        res = jnp.where(lane == b, col, res)
    sent[pl.ds(SENT - 8, 8), :] = res


def flux_kernel(se, si, ac, fx, fy, fz, flux, part, s):
    acc = [flux[i] for i in range(NP)]
    copy_rows([(s, OFF - 32, se.at[0], 0), (s, OFF + OWN, se.at[1], 0)], EDGE, 4)
    copy_rows([(s, OFF + CZ, si, 0), (s, OFF + OWN - CZ, si, INSIDE - CZ)], CZ, 4)
    acc = flux_sums(s, ac, fx, fy, fz, 0, CY, acc, before=False)
    acc = flux_sums(s, ac, fx, fy, fz, CY, 3 * CY, acc)
    acc = flux_sums(s, ac, fx, fy, fz, SLAB - 3 * CY, SLAB - CY, acc)
    acc = flux_sums(s, ac, fx, fy, fz, SLAB - CY, SLAB, acc, after=False)
    acc = crossing_sums(s, fx, -32, 0, acc)
    acc = crossing_sums(s, fx, SLAB - CY, SLAB - 32, acc)
    lane = lanes()
    res = jnp.zeros((8, CZ), F32)
    for b, col in enumerate(lane_sums(acc)):
        res = jnp.where(lane == b, col, res)
    part[...] = res


def lane_sums(acc):
    row = sublanes()
    cols = []
    for b in range(K):
        x = jnp.zeros((8, CZ), F32)
        for a in range(K):
            p = PAIRS.index((min(a, b), max(a, b)))
            x = jnp.where(row == a, jnp.sum(acc[p], axis=0, keepdims=True), x)
        cols.append(jnp.sum(x, axis=1, keepdims=True))
    return cols


GRAM = NB * K
FLUX = GRAM + K
OTHERS = FLUX + K


def couple_kernel(scal, window, near, far, part, msg, chosen, prod):
    for n in range(NB):
        m = scal[8 + n] ^ scal[3]
        place = lax.shift_right_logical(m, 1)
        odd = (m & 1) == 1
        for i in range(SLAB // CZ):
            for t in range(WMAX):
                rows = pl.ds(i * FIRST + t * K, K)
                value = jnp.where(odd, far[place, rows, :], near[place, rows, :])
                chosen[pl.ds((t * NB + n) * K, K), i * CZ : (i + 1) * CZ] = value
    prod[:, : WMAX * NB * K] = lax.dot_general(
        window[...], chosen[...], (((1,), (1,)), ((), ())), precision=HIGHEST, preferred_element_type=F32
    )
    lane = lax.broadcasted_iota(jnp.int32, (8, 2 * CZ), 1)
    total = jnp.zeros((8, 2 * CZ), F32)
    for t in range(WMAX):
        x = jnp.zeros((8, 2 * CZ), F32)
        for n in range(NB):
            width = scal[16 + n]
            d = jnp.where(t < width, WMAX - width + t, 0)
            v = prod[pl.ds(pl.multiple_of(d * K, K), K), :]
            lo = (t * NB + n) * K
            keep = (lane >= lo) & (lane < lo + K) & (t < width)
            x = jnp.where(keep, v, x)
        total = total + (pltpu.roll(x, 2 * CZ - t * NB * K, 1) if t else x)
    lane = lanes()
    res = jnp.where(lane < GRAM, total[:, :CZ], 0.0)
    res = res + pltpu.roll(part[...], FLUX, 1)
    for m in range(SUBDOMAINS):
        g = (far if m & 1 else near)[m // 2, pl.ds(SENT - 8, 8), :]
        res = res + pltpu.roll(g, OTHERS + (m - 1) * K if m else GRAM, 1)
    for i in range(msg.shape[0]):
        msg[i] = res


def eliminate(grams):
    row, lane = sublanes(), lanes()
    column = row[:, :1]
    es = []
    for g in grams:
        e = jnp.where(lane < K, g, jnp.where(lane == row + K, 1.0, 0.0))
        es.append(jnp.where(lane < 2 * K, e, 0.0))
    roots = [jnp.ones((8, 1), F32)] * len(es)
    for k in range(K):
        for m, e in enumerate(es):
            pivot = e[k : k + 1, k : k + 1]
            factor = jnp.where(column > k, e[:, k : k + 1] / pivot, 0.0)
            roots[m] = jnp.where(column == k, 1.0 / jnp.sqrt(pivot), roots[m])
            es[m] = e - factor * e[k : k + 1, :]
    return [jnp.where(lane < K, pltpu.roll(e * root, CZ - K, 1), 0.0) for e, root in zip(es, roots)]


def finish_kernel(scale, scal, got, si, se, basis, galerkin, coupling, inverse, out, sem):
    total = jnp.sum(got[...], axis=0) * scale
    (li,) = eliminate([pltpu.roll(total, CZ - GRAM, 1)])
    inverse[0] = li
    c = {(b, a): jnp.broadcast_to(li[a : a + 1, b : b + 1], (8, CZ)) for b, a in PAIRS}
    copies = []
    for i in range(SLAB // CZ):
        if i == 0:
            src = se.at[0, :, pl.ds(32, CZ)]
        elif i == SLAB // CZ - 1:
            src = se.at[1, :, pl.ds(0, CZ)]
        else:
            src = si.at[:, pl.ds((i - 1) * CZ, CZ)]

        def step(j, carry, src=src, i=i):
            stores = []
            for t in range(4):
                r = pl.multiple_of(j * 32 + t * 8, 8)
                v = [src[a, pl.ds(r, 8), :] for a in range(K)]
                for a in range(K):
                    x = c[0, a] * v[0]
                    for b in range(1, a + 1):
                        x = x + c[b, a] * v[b]
                    stores.append((a, r, x))
            for a, r, x in stores:
                out[i, a, pl.ds(r, 8), :] = x
            return carry

        lax.fori_loop(0, CZ // 32, step, 0)
        copies.append(pltpu.make_async_copy(out.at[i], basis.at[:, pl.ds(i * CZ, CZ)], sem.at[i]))
        copies[-1].start()
    others = eliminate([pltpu.roll(total, CZ - OTHERS - m * K, 1) for m in range(SUBDOMAINS - 1)])
    for m, other in enumerate(others):
        inverse[m + 1] = other
    y = jnp.dot(li[:, :K], total[:, :OTHERS], precision=HIGHEST, preferred_element_type=F32)
    transposed = (((1,), (1,)), ((), ()))
    galerkin[...] = lax.dot_general(
        y[:, FLUX:OTHERS], li[:, :K], transposed, precision=HIGHEST, preferred_element_type=F32
    )
    for n in range(NB):
        other = inverse[scal[8 + n] ^ scal[3]]
        coupling[n] = lax.dot_general(
            y[:, n * K : n * K + K], other[:, :K], transposed, precision=HIGHEST, preferred_element_type=F32
        )
    wait_all(copies)


def params(mib=40):
    return pltpu.CompilerParams(vmem_limit_bytes=mib * 1024 * 1024)


def cost(us):
    return pl.CostEstimate(flops=0, bytes_accessed=int(us * 3.0e6), transcendentals=0)


def swap(x, bits):
    return lax.ppermute(x, "subdomai", [(i, i ^ bits) for i in range(lax.axis_size("subdomai"))])


def body(start_vectors, permeability, accumulation, extents, neighbour_ids, intersection_widths):
    groups = lax.axis_size("inner")
    cells = groups * SLAB * CZ
    inner = lax.axis_index("inner")
    own = lax.axis_index("subdomai")
    sv = start_vectors.reshape(K, SLAB, CZ)
    perm = permeability.reshape(SLAB, CZ)
    acc = accumulation.reshape(SLAB, CZ)
    scal = jnp.concatenate(
        [
            extents[0],
            jnp.stack([inner * 16, own]).astype(jnp.int32),
            jnp.zeros(4, jnp.int32),
            neighbour_ids[0],
            jnp.zeros(2, jnp.int32),
            intersection_widths[0],
            jnp.zeros(10, jnp.int32),
        ]
    )
    down, up = pl.pallas_call(
        pack_kernel,
        out_shape=(shape(PACK, CZ),) * 2,
        in_specs=[HBM] * 3,
        out_specs=(VMEM,) * 2,
        scratch_shapes=[pltpu.SemaphoreType.DMA((6,))],
        compiler_params=params(60),
        name="pack",
    )(sv, perm, acc)
    right = lax.ppermute(down, "inner", [(i, (i - 1) % groups) for i in range(groups)])
    left = lax.ppermute(up, "inner", [(i, (i + 1) % groups) for i in range(groups)])
    field, plain = pltpu.VMEM((K, RT, CZ), F32), pltpu.VMEM((RT, CZ), F32)
    turning = [pltpu.VMEM((K, CZ, CZ), F32), pltpu.VMEM((CZ, CZ), F32)]
    turn = shape(FIRST, INSIDE)
    si, ve, kp, ac, fx, fy, fz, w, gram, flux, first, window = pl.pallas_call(
        interior_kernel,
        out_shape=(shape(K, INSIDE, CZ), shape(4, K, CZ, CZ))
        + (shape(RT, CZ),) * 6
        + (shape(NP, 8, CZ),) * 2
        + (turn,) * 2,
        in_specs=[SMEM, HBM, HBM, HBM],
        out_specs=(VMEM,) * 12,
        scratch_shapes=[field] * 2 + turning + [pltpu.SemaphoreType.DMA((4,))],
        compiler_params=params(36),
        cost_estimate=cost(15),
        name="interior",
    )(scal, sv, perm, acc)
    se, sent, window, fxe, fye, fze = pl.pallas_call(
        edge_kernel,
        out_shape=(shape(2, K, EDGE, CZ), shape(SENT, CZ), shape(FIRST, SLAB)) + (shape(RT, CZ),) * 3,
        in_specs=[SMEM] + [VMEM] * 12,
        out_specs=(VMEM,) * 6,
        scratch_shapes=[field] * 2 + [plain] * 3 + [pltpu.VMEM((FIRST, CZ), F32)] * 2 + turning,
        compiler_params=params(24),
        cost_estimate=cost(6),
        name="edge",
    )(scal, left, right, ve, kp, ac, fx, fy, fz, w, gram, first, window)
    moved = [swap(sent, bits) for bits in (2, 4, 6)]
    part = pl.pallas_call(
        flux_kernel,
        out_shape=shape(8, CZ),
        in_specs=[VMEM] * 7,
        out_specs=VMEM,
        scratch_shapes=[field],
        compiler_params=params(10),
        cost_estimate=cost(3),
        name="flux",
    )(se, si, ac, fxe, fye, fze, flux)
    moved, part = lax.optimization_barrier((moved, part))
    near = jnp.stack([sent] + moved)
    far = swap(near, 1)
    msg = pl.pallas_call(
        couple_kernel,
        out_shape=shape(groups, 8, CZ),
        in_specs=[SMEM] + [VMEM] * 4,
        out_specs=VMEM,
        scratch_shapes=[pltpu.VMEM((WMAX * NB * K, SLAB), F32), pltpu.VMEM((FIRST, 2 * CZ), F32)],
        compiler_params=params(8),
        cost_estimate=cost(1),
        name="couple",
    )(scal, window, near, far, part)
    got = lax.all_to_all(msg, "inner", 0, 0)
    basis, galerkin, coupling = pl.pallas_call(
        functools.partial(finish_kernel, 1.0 / cells),
        out_shape=(shape(K, SLAB, CZ), shape(K, K), shape(NB, K, K)),
        in_specs=[SMEM] + [VMEM] * 3,
        out_specs=(HBM, VMEM, VMEM),
        scratch_shapes=[
            pltpu.VMEM((SUBDOMAINS, 8, CZ), F32),
            pltpu.VMEM((SLAB // CZ, K, CZ, CZ), F32),
            pltpu.SemaphoreType.DMA((SLAB // CZ,)),
        ],
        compiler_params=params(8),
        cost_estimate=cost(5),
        name="finish",
    )(scal, got, si, se)
    return basis.reshape(start_vectors.shape), galerkin[None], coupling[None]


def solution(mesh):
    return jax.shard_map(
        body,
        mesh=mesh,
        in_specs=(
            P(None, ("subdomai", "inner"), None, None),
            P(("subdomai", "inner"), None, None),
            P(("subdomai", "inner"), None, None),
            P("subdomai", None),
            P("subdomai", None),
            P("subdomai", None),
        ),
        out_specs=(
            P(None, ("subdomai", "inner"), None, None),
            P("subdomai", None, None),
            P("subdomai", None, None, None),
        ),
        check_vma=False,
    )
```

```python
import functools
import jax
import jax.numpy as jnp
from jax import lax
from jax.experimental import pallas as pl
from jax.experimental.pallas import tpu as pltpu
from jax.sharding import PartitionSpec as P

F32 = jnp.float32
K = 8
NB = 6
SUBDOMAINS = 8
WMAX = 4
CY = 64
CZ = 128
OMEGA = 0.6
SLAB = 16 * CY
HALO = 160
HALO_ACC = 96
OFF = HALO + 8
RT = SLAB + 2 * OFF
PACK = K * HALO + HALO + HALO_ACC
PAIRS = [(a, b) for b in range(K) for a in range(b + 1)]
NP = len(PAIRS)
BY_MATRIX = 4
HIGHEST = lax.Precision.HIGHEST
VMEM = pl.BlockSpec(memory_space=pltpu.VMEM)
SMEM = pl.BlockSpec(memory_space=pltpu.SMEM)
HBM = pl.BlockSpec(memory_space=pltpu.HBM)
ANY = pl.BlockSpec(memory_space=pl.ANY)


def shape(*dims):
    return jax.ShapeDtypeStruct(dims, F32)


def aligned(x, n):
    return x if isinstance(x, int) else pl.multiple_of(x, n)


def loop(lo, hi, step, init):
    return step(lo, init) if hi - lo == 1 else lax.fori_loop(lo, hi, step, init)


def rows_loop(lo, hi, step, init=(), tiles=4):
    def one(i, carry):
        stores = []
        for j in range(tiles):
            more, carry = step(aligned(lo + OFF + (i * tiles + j) * 8, 8), carry)
            stores += more
        for ref, place, value in stores:
            ref[place] = value
        return carry

    assert (hi - lo) % (8 * tiles) == 0
    return loop(0, (hi - lo) // (8 * tiles), one, init)


def tile_at(row):
    return (pl.ds(row, 8), slice(None))


def field_at(a, row):
    return (a, pl.ds(row, 8), slice(None))


def lanes():
    return lax.broadcasted_iota(jnp.int32, (8, CZ), 1)


def sublanes():
    return lax.broadcasted_iota(jnp.int32, (8, CZ), 0)


def at(ref, row):
    return ref[pl.ds(row, 8), :]


def fat(ref, a, row):
    return ref[a, pl.ds(row, 8), :]


def layer_of(row):
    return ((row + (192 - OFF)) >> 6) - 3


def active(scal, row, more=0):
    x = scal[2] + layer_of(row) + more
    return jnp.where((x >= 0) & (x < scal[0]), 1.0, 0.0).astype(F32)


def faces(scal, kp, fx, fy, fz, lo, hi, tiles=8):
    mz = jnp.where(lanes() < scal[1], 2.0, 0.0).astype(F32)
    mzz = jnp.where(lanes() < scal[1] - 1, 2.0, 0.0).astype(F32)
    sub = sublanes()

    def step(r, carry):
        here = active(scal, r)
        there = active(scal, r, 1)
        k = at(kp, r)
        kx = at(kp, r + CY)
        ky = at(kp, r + 1)
        kz = pltpu.roll(k, CZ - 1, 1)
        inside = jnp.where(((r + (192 - OFF)) & (CY - 1)) == CY - 8, 0.0, 1.0).astype(F32)
        my = jnp.where(sub == 7, inside, 1.0)
        stores = [
            (fx, tile_at(r), (mz * (here * there)) * k * kx / (k + kx)),
            (fy, tile_at(r), (mz * here) * my * k * ky / (k + ky)),
            (fz, tile_at(r), (mzz * here) * k * kz / (k + kz)),
        ]
        return stores, carry

    rows_loop(lo, hi, step, tiles=tiles)


def weights(ac, fx, fy, fz, w, lo, hi, tiles=8):
    def step(r, carry):
        z = at(fz, r)
        diagonal = (
            (at(ac, r) + at(fx, r))
            + (at(fx, r - CY) + at(fy, r))
            + (at(fy, r - 1) + z)
            + pltpu.roll(z, 1, 1)
        )
        return [(w, tile_at(r), OMEGA / diagonal)], carry

    rows_loop(lo, hi, step, tiles=tiles)


def pieces(v):
    high = v.astype(jnp.bfloat16)
    return high, (v - high.astype(F32)).astype(jnp.bfloat16)


def shifter():
    row = lax.broadcasted_iota(jnp.int32, (2 * CZ, 2 * CZ), 0) & (CZ - 1)
    col = lax.broadcasted_iota(jnp.int32, (2 * CZ, 2 * CZ), 1)
    source = jnp.where(col < CZ, col + 1, col + CZ - 1) & (CZ - 1)
    return jnp.where(row == source, 1.0, 0.0).astype(F32).astype(jnp.bfloat16)


def smooth(scal, src, dst, fx, fy, fz, w, lo, hi, masked, tiles=16, back=0, by_matrix=BY_MATRIX):
    mz = jnp.where(lanes() < scal[1], 1.0 - OMEGA, 0.0).astype(F32)
    shift = shifter()

    def step(i, carry):
        top = aligned(lo + OFF + i * tiles * 8, 8)
        moved = {}
        for a in range(by_matrix):
            v = src[a, pl.ds(top, tiles * 8), :]
            moved[a] = jnp.dot(jnp.concatenate(pieces(v), axis=1), shift, preferred_element_type=F32)
        stores = []
        for j in range(tiles):
            r = aligned(top + j * 8, 8)
            wt = at(w, r)
            z = at(fz, r)
            xp = wt * at(fx, r)
            xm = wt * at(fx, r - CY)
            yp = wt * at(fy, r)
            ym = wt * at(fy, r - 1)
            zp = wt * z
            zm = wt * pltpu.roll(z, 1, 1)
            centre = mz * active(scal, r) if masked else 1.0 - OMEGA
            for a in range(K):
                v = fat(src, a, r)
                if a in moved:
                    after = moved[a][j * 8 : j * 8 + 8, :CZ]
                    before = moved[a][j * 8 : j * 8 + 8, CZ:]
                else:
                    after = pltpu.roll(v, CZ - 1, 1)
                    before = pltpu.roll(v, 1, 1)
                new = (
                    (centre * v + xp * fat(src, a, r + CY))
                    + (xm * fat(src, a, r - CY) + yp * fat(src, a, r + 1))
                    + (ym * fat(src, a, r - 1) + zp * after)
                    + zm * before
                )
                stores.append((dst, field_at(a, r - back), new))
        for ref, place, value in stores:
            ref[place] = value
        return carry

    assert (hi - lo) % (8 * tiles) == 0
    loop(0, (hi - lo) // (8 * tiles), step, 0)


def gram_sums(s, lo, hi, acc, back=0):
    def step(r, acc):
        v = [fat(s, a, r - back) for a in range(K)]
        return [], tuple(t + v[a] * v[b] for t, (a, b) in zip(acc, PAIRS))

    return rows_loop(lo, hi, step, tuple(acc), tiles=8)


def flux_sums(s, ac, fx, fy, fz, lo, hi, acc, before=True, after=True, back=0):
    def step(r, acc):
        out = list(acc)
        z = at(fz, r)
        xp = at(fx, r)
        xm = at(fx, r - CY)
        yp = at(fy, r)
        ym = at(fy, r - 1)
        d = at(ac, r)
        q = r - back
        v = [fat(s, a, q) for a in range(K)]
        g = [c - pltpu.roll(c, CZ - 1, 1) for c in v]
        for b in range(K):
            c = v[b]
            image = d * c + yp * (c - fat(s, b, q + 1)) + ym * (c - fat(s, b, q - 1))
            if after:
                image = image + xp * (c - fat(s, b, q + CY))
            if before:
                image = image + xm * (c - fat(s, b, q - CY))
            down = z * g[b]
            for a in range(b + 1):
                p = b * (b + 1) // 2 + a
                out[p] = out[p] + (v[a] * image + g[a] * down)
        return [], tuple(out)

    return rows_loop(lo, hi, step, tuple(acc), tiles=4)


def crossing_sums(s, fx, lo, hi, acc):
    def step(r, acc):
        f = at(fx, r)
        d = [fat(s, a, r) - fat(s, a, r + CY) for a in range(K)]
        e = [f * t for t in d]
        return [], tuple(t + d[a] * e[b] for t, (a, b) in zip(acc, PAIRS))

    return rows_loop(lo, hi, step, tuple(acc), tiles=1)


def turned(scal, s, kp, first, window, tile, ptile, blocks, back=0):
    start = scal[1] - WMAX

    def step(block, row, lane):
        ptile[...] = kp[pl.ds(row, CZ), :].T
        kw = ptile[pl.ds(start, WMAX), :]
        for a in range(K):
            tile[a] = s[a, pl.ds(aligned(row - back, 8), CZ), :].T
        for a in range(K):
            u = tile[a, pl.ds(start, WMAX), :] * kw
            f = tile[a, pl.ds(0, WMAX), :]
            for t in range(WMAX):
                first[pl.ds(t * K + a, 1), pl.ds(lane, CZ)] = f[t : t + 1]
                window[pl.ds(t * K + a, 1), pl.ds(lane, CZ)] = u[t : t + 1]

    def one(block, carry):
        step(block, aligned(OFF + block * CZ, 8), aligned((block - blocks[0]) * CZ, CZ))
        return carry

    loop(blocks[0], blocks[1], one, 0)


def copy_all(pairs, sem):
    copies = [pltpu.make_async_copy(src, dst, sem.at[i]) for i, (src, dst) in enumerate(pairs)]
    for c in copies:
        c.start()
    return copies


def wait_all(copies):
    for c in copies:
        c.wait()


def pack_kernel(sv, perm, acc, down, up, sem):
    pairs = []
    for out, lo, acc_lo in ((down, 0, 0), (up, SLAB - HALO, SLAB - HALO_ACC)):
        pairs.append((sv.at[:, pl.ds(lo, HALO)], out.at[pl.ds(0, K * HALO)].reshape(K, HALO, CZ)))
        pairs.append((perm.at[pl.ds(lo, HALO)], out.at[pl.ds(K * HALO, HALO)]))
        pairs.append((acc.at[pl.ds(acc_lo, HALO_ACC)], out.at[pl.ds((K + 1) * HALO, HALO_ACC)]))
    wait_all(copy_all(pairs, sem))


INSIDE = SLAB - 4 * CY
EDGE = 2 * CY + 32
FIRST = WMAX * K
SENT = SLAB // CZ * FIRST + 8


BACK = OFF + 2 * CY
OWN = SLAB - CZ
EDGE_BACK = (OFF - 32, OFF + OWN)


def copy_rows(moves, count, group):
    def one(i, carry):
        values = []
        for j in range(group):
            for dst, at_dst, src, at_src in moves:
                rows = [pl.ds(aligned(r + (i * group + j) * 8, 8), 8) for r in (at_dst, at_src)]
                if len(dst.shape) == 2:
                    values.append((dst, (rows[0], slice(None)), src[rows[1], :]))
                else:
                    for a in range(K):
                        values.append((dst, (a, rows[0], slice(None)), src[a, rows[1], :]))
        for dst, place, value in values:
            dst[place] = value
        return carry

    assert count % (8 * group) == 0
    loop(0, count // (8 * group), one, 0)


def interior_kernel(
    scal, sv, perm, acc, si, ve, kp, ac, fx, fy, fz, w, gram, flux, first, window, v0, v1, tile, ptile, sem
):
    slab = pl.ds(OFF, SLAB)
    a, b, c = copy_all([(perm, kp.at[slab]), (acc, ac.at[slab]), (sv, v0.at[:, slab])], sem)
    a.wait()
    faces(scal, kp, fx, fy, fz, 0, SLAB - CY, 20)
    b.wait()
    weights(ac, fx, fy, fz, w, CY, SLAB - CY, 16)
    c.wait()
    smooth(scal, v0, v1, fx, fy, fz, w, CY, SLAB - CY, True)
    out = copy_all(
        [
            (v0.at[:, pl.ds(OFF, CZ)], ve.at[0]),
            (v0.at[:, pl.ds(OFF + OWN, CZ)], ve.at[1]),
            (v1.at[:, pl.ds(OFF + CY, CZ)], ve.at[2]),
            (v1.at[:, pl.ds(OFF + SLAB - CY - CZ, CZ)], ve.at[3]),
        ],
        sem,
    )
    smooth(scal, v1, si, fx, fy, fz, w, 2 * CY, SLAB - 2 * CY, False, back=BACK)
    zero = [jnp.zeros((8, CZ), F32)] * NP
    for i, t in enumerate(gram_sums(si, 2 * CY, SLAB - 2 * CY, zero, back=BACK)):
        gram[i] = t
    for i, t in enumerate(flux_sums(si, ac, fx, fy, fz, 3 * CY, SLAB - 3 * CY, zero, back=BACK)):
        flux[i] = t
    turned(scal, si, kp, first, window, tile, ptile, (1, 7), back=BACK)
    wait_all(out)


def edge_kernel(
    scal, left, right, ve, kpi, aci, fxi, fyi, fzi, wi, gram, firsti, windowi,
    se, sent, window, fx, fy, fz, v0, v1, kp, ac, w, fe, we, tile, ptile,
):
    ends = ((left, -HALO, -HALO_ACC, 0), (right, SLAB, SLAB, OWN))
    moves = [(kp, OFF + lo, src, K * HALO) for src, lo, _, _ in ends]
    copy_rows(moves, HALO, 20)
    moves = [(ac, OFF + lo, src, (K + 1) * HALO) for src, _, lo, _ in ends]
    copy_rows(moves, HALO_ACC, 12)
    copy_rows([(new, OFF + n, old, OFF + n) for new, old in ((kp, kpi), (ac, aci)) for n in (0, OWN)], CZ, 16)
    both = (0, SLAB - 4 * CY)
    copy_rows([(new, OFF + n, old, OFF + n) for new, old in ((fx, fxi), (fy, fyi), (fz, fzi)) for n in both], 3 * CY, 8)
    copy_rows([(w, OFF + n, wi, OFF + n) for n in (CY, SLAB - 2 * CY)], CY, 8)
    faces(scal, kp, fx, fy, fz, -HALO, 0, 20)
    faces(scal, kp, fx, fy, fz, SLAB - CY, SLAB + HALO_ACC, 20)
    weights(ac, fx, fy, fz, w, -HALO_ACC, CY, 20)
    weights(ac, fx, fy, fz, w, SLAB - CY, SLAB + HALO_ACC, 20)
    for src, lo, _, _ in ends:
        for a in range(K):
            copy_rows([(v0.at[a], OFF + lo, src, a * HALO)], HALO, 20)
    for i, near in enumerate((0, OWN)):
        copy_rows([(v0, OFF + near, ve.at[i], 0)], CZ, 8)
    for i, near in enumerate((CY, SLAB - CY - CZ)):
        copy_rows([(v1, OFF + near, ve.at[2 + i], 0)], CZ, 8)
    smooth(scal, v0, v1, fx, fy, fz, w, -HALO_ACC, CY, True, 20)
    smooth(scal, v0, v1, fx, fy, fz, w, SLAB - CY, SLAB + HALO_ACC, True, 20)
    smooth(scal, v1, se.at[0], fx, fy, fz, w, -32, 2 * CY, False, 20, EDGE_BACK[0])
    smooth(scal, v1, se.at[1], fx, fy, fz, w, SLAB - 2 * CY, SLAB + 32, False, 20, EDGE_BACK[1])
    window[:, pl.ds(CZ, INSIDE)] = windowi[...]
    for i in range(INSIDE // CZ):
        sent[pl.ds((i + 1) * FIRST, FIRST), :] = firsti[:, i * CZ : (i + 1) * CZ]
    for i, lane, end in ((0, 0, 0), (7, OWN, 1)):
        turned(scal, se.at[end], kp, fe, we, tile, ptile, (i, i + 1), EDGE_BACK[end])
        sent[pl.ds(i * FIRST, FIRST), :] = fe[...]
        window[:, pl.ds(lane, CZ)] = we[...]
    acc = [gram[i] for i in range(NP)]
    acc = gram_sums(se.at[0], 0, 2 * CY, acc, EDGE_BACK[0])
    acc = gram_sums(se.at[1], SLAB - 2 * CY, SLAB, acc, EDGE_BACK[1])
    lane = lanes()
    res = jnp.zeros((8, CZ), F32)
    for b, col in enumerate(lane_sums(acc)):
        res = jnp.where(lane == b, col, res)
    sent[pl.ds(SENT - 8, 8), :] = res


def flux_kernel(se, si, ac, fx, fy, fz, flux, part, s):
    acc = [flux[i] for i in range(NP)]
    copy_rows([(s, OFF - 32, se.at[0], 0), (s, OFF + OWN, se.at[1], 0)], EDGE, 4)
    copy_rows([(s, OFF + CZ, si, 0), (s, OFF + OWN - CZ, si, INSIDE - CZ)], CZ, 4)
    acc = flux_sums(s, ac, fx, fy, fz, 0, CY, acc, before=False)
    acc = flux_sums(s, ac, fx, fy, fz, CY, 3 * CY, acc)
    acc = flux_sums(s, ac, fx, fy, fz, SLAB - 3 * CY, SLAB - CY, acc)
    acc = flux_sums(s, ac, fx, fy, fz, SLAB - CY, SLAB, acc, after=False)
    acc = crossing_sums(s, fx, -32, 0, acc)
    acc = crossing_sums(s, fx, SLAB - CY, SLAB - 32, acc)
    lane = lanes()
    res = jnp.zeros((8, CZ), F32)
    for b, col in enumerate(lane_sums(acc)):
        res = jnp.where(lane == b, col, res)
    part[...] = res


def lane_sums(acc):
    row = sublanes()
    cols = []
    for b in range(K):
        x = jnp.zeros((8, CZ), F32)
        for a in range(K):
            p = PAIRS.index((min(a, b), max(a, b)))
            x = jnp.where(row == a, jnp.sum(acc[p], axis=0, keepdims=True), x)
        cols.append(jnp.sum(x, axis=1, keepdims=True))
    return cols


GRAM = NB * K
FLUX = GRAM + K
OTHERS = FLUX + K


def couple_kernel(scal, window, near, far, part, msg, chosen, prod):
    for n in range(NB):
        m = scal[8 + n] ^ scal[3]
        place = lax.shift_right_logical(m, 1)
        odd = (m & 1) == 1
        for i in range(SLAB // CZ):
            for t in range(WMAX):
                rows = pl.ds(i * FIRST + t * K, K)
                value = jnp.where(odd, far[place, rows, :], near[place, rows, :])
                chosen[pl.ds((t * NB + n) * K, K), i * CZ : (i + 1) * CZ] = value
    mine, mine_low = pieces(window[...])
    theirs, theirs_low = pieces(chosen[...])
    both = (((1,), (1,)), ((), ()))
    prod[:, : WMAX * NB * K] = (
        lax.dot_general(mine, theirs_low, both, preferred_element_type=F32)
        + lax.dot_general(mine_low, theirs, both, preferred_element_type=F32)
    ) + lax.dot_general(mine, theirs, both, preferred_element_type=F32)
    lane = lax.broadcasted_iota(jnp.int32, (8, 2 * CZ), 1)
    total = jnp.zeros((8, 2 * CZ), F32)
    for t in range(WMAX):
        x = jnp.zeros((8, 2 * CZ), F32)
        for n in range(NB):
            width = scal[16 + n]
            d = jnp.where(t < width, WMAX - width + t, 0)
            v = prod[pl.ds(pl.multiple_of(d * K, K), K), :]
            lo = (t * NB + n) * K
            keep = (lane >= lo) & (lane < lo + K) & (t < width)
            x = jnp.where(keep, v, x)
        total = total + (pltpu.roll(x, 2 * CZ - t * NB * K, 1) if t else x)
    lane = lanes()
    res = jnp.where(lane < GRAM, total[:, :CZ], 0.0)
    res = res + pltpu.roll(part[...], FLUX, 1)
    for m in range(SUBDOMAINS):
        g = (far if m & 1 else near)[m // 2, pl.ds(SENT - 8, 8), :]
        res = res + pltpu.roll(g, OTHERS + (m - 1) * K if m else GRAM, 1)
    for i in range(msg.shape[0]):
        msg[i] = res


def eliminate(grams):
    row, lane = sublanes(), lanes()
    column = row[:, :1]
    es = []
    for g in grams:
        e = jnp.where(lane < K, g, jnp.where(lane == row + K, 1.0, 0.0))
        es.append(jnp.where(lane < 2 * K, e, 0.0))
    roots = [jnp.ones((8, 1), F32)] * len(es)
    for k in range(K):
        for m, e in enumerate(es):
            pivot = e[k : k + 1, k : k + 1]
            factor = jnp.where(column > k, e[:, k : k + 1] / pivot, 0.0)
            roots[m] = jnp.where(column == k, 1.0 / jnp.sqrt(pivot), roots[m])
            es[m] = e - factor * e[k : k + 1, :]
    return [jnp.where(lane < K, pltpu.roll(e * root, CZ - K, 1), 0.0) for e, root in zip(es, roots)]


def finish_kernel(scale, scal, got, si, se, basis, galerkin, coupling, inverse, out, sem):
    total = jnp.sum(got[...], axis=0) * scale
    (li,) = eliminate([pltpu.roll(total, CZ - GRAM, 1)])
    inverse[0] = li
    c = {(b, a): jnp.broadcast_to(li[a : a + 1, b : b + 1], (8, CZ)) for b, a in PAIRS}
    copies = []
    for i in range(SLAB // CZ):
        if i == 0:
            src = se.at[0, :, pl.ds(32, CZ)]
        elif i == SLAB // CZ - 1:
            src = se.at[1, :, pl.ds(0, CZ)]
        else:
            src = si.at[:, pl.ds((i - 1) * CZ, CZ)]

        def step(j, carry, src=src, i=i):
            stores = []
            for t in range(8):
                r = pl.multiple_of(j * 64 + t * 8, 8)
                v = [src[a, pl.ds(r, 8), :] for a in range(K)]
                for a in range(K):
                    x = c[0, a] * v[0]
                    for b in range(1, a + 1):
                        x = x + c[b, a] * v[b]
                    stores.append((a, r, x))
            for a, r, x in stores:
                out[i, a, pl.ds(r, 8), :] = x
            return carry

        lax.fori_loop(0, CZ // 64, step, 0)
        copies.append(pltpu.make_async_copy(out.at[i], basis.at[:, pl.ds(i * CZ, CZ)], sem.at[i]))
        copies[-1].start()
    others = eliminate([pltpu.roll(total, CZ - OTHERS - m * K, 1) for m in range(SUBDOMAINS - 1)])
    for m, other in enumerate(others):
        inverse[m + 1] = other
    y = jnp.dot(li[:, :K], total[:, :OTHERS], precision=HIGHEST, preferred_element_type=F32)
    transposed = (((1,), (1,)), ((), ()))
    galerkin[...] = lax.dot_general(
        y[:, FLUX:OTHERS], li[:, :K], transposed, precision=HIGHEST, preferred_element_type=F32
    )
    for n in range(NB):
        other = inverse[scal[8 + n] ^ scal[3]]
        coupling[n] = lax.dot_general(
            y[:, n * K : n * K + K], other[:, :K], transposed, precision=HIGHEST, preferred_element_type=F32
        )
    wait_all(copies)


def params(mib=40):
    return pltpu.CompilerParams(vmem_limit_bytes=mib * 1024 * 1024)


def cost(us):
    return pl.CostEstimate(flops=0, bytes_accessed=int(us * 3.0e6), transcendentals=0)


def swap(x, bits):
    return lax.ppermute(x, "subdomai", [(i, i ^ bits) for i in range(lax.axis_size("subdomai"))])


def body(start_vectors, permeability, accumulation, extents, neighbour_ids, intersection_widths):
    groups = lax.axis_size("inner")
    cells = groups * SLAB * CZ
    inner = lax.axis_index("inner")
    own = lax.axis_index("subdomai")
    sv = start_vectors.reshape(K, SLAB, CZ)
    perm = permeability.reshape(SLAB, CZ)
    acc = accumulation.reshape(SLAB, CZ)
    scal = jnp.concatenate(
        [
            extents[0],
            jnp.stack([inner * 16, own]).astype(jnp.int32),
            jnp.zeros(4, jnp.int32),
            neighbour_ids[0],
            jnp.zeros(2, jnp.int32),
            intersection_widths[0],
            jnp.zeros(10, jnp.int32),
        ]
    )
    down, up = pl.pallas_call(
        pack_kernel,
        out_shape=(shape(PACK, CZ),) * 2,
        in_specs=[HBM] * 3,
        out_specs=(VMEM,) * 2,
        scratch_shapes=[pltpu.SemaphoreType.DMA((6,))],
        compiler_params=params(60),
        name="pack",
    )(sv, perm, acc)
    right = lax.ppermute(down, "inner", [(i, (i - 1) % groups) for i in range(groups)])
    left = lax.ppermute(up, "inner", [(i, (i + 1) % groups) for i in range(groups)])
    field, plain = pltpu.VMEM((K, RT, CZ), F32), pltpu.VMEM((RT, CZ), F32)
    turning = [pltpu.VMEM((K, CZ, CZ), F32), pltpu.VMEM((CZ, CZ), F32)]
    turn = shape(FIRST, INSIDE)
    si, ve, kp, ac, fx, fy, fz, w, gram, flux, first, window = pl.pallas_call(
        interior_kernel,
        out_shape=(shape(K, INSIDE, CZ), shape(4, K, CZ, CZ))
        + (shape(RT, CZ),) * 6
        + (shape(NP, 8, CZ),) * 2
        + (turn,) * 2,
        in_specs=[SMEM, HBM, HBM, HBM],
        out_specs=(VMEM,) * 12,
        scratch_shapes=[field] * 2 + turning + [pltpu.SemaphoreType.DMA((4,))],
        compiler_params=params(36),
        cost_estimate=cost(15),
        name="interior",
    )(scal, sv, perm, acc)
    se, sent, window, fxe, fye, fze = pl.pallas_call(
        edge_kernel,
        out_shape=(shape(2, K, EDGE, CZ), shape(SENT, CZ), shape(FIRST, SLAB)) + (shape(RT, CZ),) * 3,
        in_specs=[SMEM] + [VMEM] * 12,
        out_specs=(VMEM,) * 6,
        scratch_shapes=[field] * 2 + [plain] * 3 + [pltpu.VMEM((FIRST, CZ), F32)] * 2 + turning,
        compiler_params=params(24),
        cost_estimate=cost(6),
        name="edge",
    )(scal, left, right, ve, kp, ac, fx, fy, fz, w, gram, first, window)
    moved = [swap(sent, bits) for bits in (2, 4, 6)]
    part = pl.pallas_call(
        flux_kernel,
        out_shape=shape(8, CZ),
        in_specs=[VMEM] * 7,
        out_specs=VMEM,
        scratch_shapes=[field],
        compiler_params=params(10),
        cost_estimate=cost(3),
        name="flux",
    )(se, si, ac, fxe, fye, fze, flux)
    moved, part = lax.optimization_barrier((moved, part))
    near = jnp.stack([sent] + moved)
    far = swap(near, 1)
    msg = pl.pallas_call(
        couple_kernel,
        out_shape=shape(groups, 8, CZ),
        in_specs=[SMEM] + [VMEM] * 4,
        out_specs=VMEM,
        scratch_shapes=[pltpu.VMEM((WMAX * NB * K, SLAB), F32), pltpu.VMEM((FIRST, 2 * CZ), F32)],
        compiler_params=params(8),
        cost_estimate=cost(1),
        name="couple",
    )(scal, window, near, far, part)
    got = lax.all_to_all(msg, "inner", 0, 0)
    basis, galerkin, coupling = pl.pallas_call(
        functools.partial(finish_kernel, 1.0 / cells),
        out_shape=(shape(K, SLAB, CZ), shape(K, K), shape(NB, K, K)),
        in_specs=[SMEM] + [VMEM] * 3,
        out_specs=(HBM, VMEM, VMEM),
        scratch_shapes=[
            pltpu.VMEM((SUBDOMAINS, 8, CZ), F32),
            pltpu.VMEM((SLAB // CZ, K, CZ, CZ), F32),
            pltpu.SemaphoreType.DMA((SLAB // CZ,)),
        ],
        compiler_params=params(8),
        cost_estimate=cost(5),
        name="finish",
    )(scal, got, si, se)
    return basis.reshape(start_vectors.shape), galerkin[None], coupling[None]


def solution(mesh):
    return jax.shard_map(
        body,
        mesh=mesh,
        in_specs=(
            P(None, ("subdomai", "inner"), None, None),
            P(("subdomai", "inner"), None, None),
            P(("subdomai", "inner"), None, None),
            P("subdomai", None),
            P("subdomai", None),
            P("subdomai", None),
        ),
        out_specs=(
            P(None, ("subdomai", "inner"), None, None),
            P("subdomai", None, None),
            P("subdomai", None, None, None),
        ),
        check_vma=False,
    )
```

```python
import functools
import jax
import jax.numpy as jnp
from jax import lax
from jax.experimental import pallas as pl
from jax.experimental.pallas import tpu as pltpu
from jax.sharding import PartitionSpec as P

F32 = jnp.float32
K = 8
NB = 6
SUBDOMAINS = 8
WMAX = 4
CY = 64
CZ = 128
OMEGA = 0.6
SLAB = 16 * CY
HALO = 160
HALO_ACC = 96
OFF = HALO + 8
RT = SLAB + 2 * OFF
PACK = K * HALO + HALO + HALO_ACC
PAIRS = [(a, b) for b in range(K) for a in range(b + 1)]
NP = len(PAIRS)
BY_MATRIX = 4
HIGHEST = lax.Precision.HIGHEST
VMEM = pl.BlockSpec(memory_space=pltpu.VMEM)
SMEM = pl.BlockSpec(memory_space=pltpu.SMEM)
HBM = pl.BlockSpec(memory_space=pltpu.HBM)
ANY = pl.BlockSpec(memory_space=pl.ANY)


def shape(*dims):
    return jax.ShapeDtypeStruct(dims, F32)


def aligned(x, n):
    return x if isinstance(x, int) else pl.multiple_of(x, n)


def loop(lo, hi, step, init):
    return step(lo, init) if hi - lo == 1 else lax.fori_loop(lo, hi, step, init)


def rows_loop(lo, hi, step, init=(), tiles=4):
    def one(i, carry):
        stores = []
        for j in range(tiles):
            more, carry = step(aligned(lo + OFF + (i * tiles + j) * 8, 8), carry)
            stores += more
        for ref, place, value in stores:
            ref[place] = value
        return carry

    assert (hi - lo) % (8 * tiles) == 0
    return loop(0, (hi - lo) // (8 * tiles), one, init)


def tile_at(row):
    return (pl.ds(row, 8), slice(None))


def field_at(a, row):
    return (a, pl.ds(row, 8), slice(None))


def lanes():
    return lax.broadcasted_iota(jnp.int32, (8, CZ), 1)


def sublanes():
    return lax.broadcasted_iota(jnp.int32, (8, CZ), 0)


def at(ref, row):
    return ref[pl.ds(row, 8), :]


def fat(ref, a, row):
    return ref[a, pl.ds(row, 8), :]


def layer_of(row):
    return ((row + (192 - OFF)) >> 6) - 3


def active(scal, row, more=0):
    x = scal[2] + layer_of(row) + more
    return jnp.where((x >= 0) & (x < scal[0]), 1.0, 0.0).astype(F32)


def faces(scal, kp, fx, fy, fz, lo, hi, tiles=8):
    mz = jnp.where(lanes() < scal[1], 2.0, 0.0).astype(F32)
    mzz = jnp.where(lanes() < scal[1] - 1, 2.0, 0.0).astype(F32)
    sub = sublanes()

    def step(r, carry):
        here = active(scal, r)
        there = active(scal, r, 1)
        k = at(kp, r)
        kx = at(kp, r + CY)
        ky = at(kp, r + 1)
        kz = pltpu.roll(k, CZ - 1, 1)
        inside = jnp.where(((r + (192 - OFF)) & (CY - 1)) == CY - 8, 0.0, 1.0).astype(F32)
        my = jnp.where(sub == 7, inside, 1.0)
        stores = [
            (fx, tile_at(r), (mz * (here * there)) * k * kx / (k + kx)),
            (fy, tile_at(r), (mz * here) * my * k * ky / (k + ky)),
            (fz, tile_at(r), (mzz * here) * k * kz / (k + kz)),
        ]
        return stores, carry

    rows_loop(lo, hi, step, tiles=tiles)


def weights(ac, fx, fy, fz, w, lo, hi, tiles=8):
    def step(r, carry):
        z = at(fz, r)
        diagonal = (
            (at(ac, r) + at(fx, r))
            + (at(fx, r - CY) + at(fy, r))
            + (at(fy, r - 1) + z)
            + pltpu.roll(z, 1, 1)
        )
        return [(w, tile_at(r), OMEGA / diagonal)], carry

    rows_loop(lo, hi, step, tiles=tiles)


def pieces(v):
    high = v.astype(jnp.bfloat16)
    return high, (v - high.astype(F32)).astype(jnp.bfloat16)


def shifter():
    row = lax.broadcasted_iota(jnp.int32, (2 * CZ, 2 * CZ), 0) & (CZ - 1)
    col = lax.broadcasted_iota(jnp.int32, (2 * CZ, 2 * CZ), 1)
    source = jnp.where(col < CZ, col + 1, col + CZ - 1) & (CZ - 1)
    return jnp.where(row == source, 1.0, 0.0).astype(F32).astype(jnp.bfloat16)


def smooth(scal, src, dst, fx, fy, fz, w, lo, hi, masked, tiles=16, back=0, by_matrix=BY_MATRIX):
    mz = jnp.where(lanes() < scal[1], 1.0 - OMEGA, 0.0).astype(F32)
    shift = shifter()

    def step(i, carry):
        top = aligned(lo + OFF + i * tiles * 8, 8)
        moved = {}
        for a in range(by_matrix):
            v = src[a, pl.ds(top, tiles * 8), :]
            moved[a] = jnp.dot(jnp.concatenate(pieces(v), axis=1), shift, preferred_element_type=F32)
        stores = []
        for j in range(tiles):
            r = aligned(top + j * 8, 8)
            wt = at(w, r)
            z = at(fz, r)
            xp = wt * at(fx, r)
            xm = wt * at(fx, r - CY)
            yp = wt * at(fy, r)
            ym = wt * at(fy, r - 1)
            zp = wt * z
            zm = wt * pltpu.roll(z, 1, 1)
            centre = mz * active(scal, r) if masked else 1.0 - OMEGA
            for a in range(K):
                v = fat(src, a, r)
                if a in moved:
                    after = moved[a][j * 8 : j * 8 + 8, :CZ]
                    before = moved[a][j * 8 : j * 8 + 8, CZ:]
                else:
                    after = pltpu.roll(v, CZ - 1, 1)
                    before = pltpu.roll(v, 1, 1)
                new = (
                    (centre * v + xp * fat(src, a, r + CY))
                    + (xm * fat(src, a, r - CY) + yp * fat(src, a, r + 1))
                    + (ym * fat(src, a, r - 1) + zp * after)
                    + zm * before
                )
                stores.append((dst, field_at(a, r - back), new))
        for ref, place, value in stores:
            ref[place] = value
        return carry

    assert (hi - lo) % (8 * tiles) == 0
    loop(0, (hi - lo) // (8 * tiles), step, 0)


def gram_sums(s, lo, hi, acc, back=0):
    def step(r, acc):
        v = [fat(s, a, r - back) for a in range(K)]
        return [], tuple(t + v[a] * v[b] for t, (a, b) in zip(acc, PAIRS))

    return rows_loop(lo, hi, step, tuple(acc), tiles=8)


def flux_sums(s, ac, fx, fy, fz, lo, hi, acc, before=True, after=True, back=0):
    def step(r, acc):
        out = list(acc)
        z = at(fz, r)
        xp = at(fx, r)
        xm = at(fx, r - CY)
        yp = at(fy, r)
        ym = at(fy, r - 1)
        d = at(ac, r)
        q = r - back
        v = [fat(s, a, q) for a in range(K)]
        g = [c - pltpu.roll(c, CZ - 1, 1) for c in v]
        for b in range(K):
            c = v[b]
            image = d * c + yp * (c - fat(s, b, q + 1)) + ym * (c - fat(s, b, q - 1))
            if after:
                image = image + xp * (c - fat(s, b, q + CY))
            if before:
                image = image + xm * (c - fat(s, b, q - CY))
            down = z * g[b]
            for a in range(b + 1):
                p = b * (b + 1) // 2 + a
                out[p] = out[p] + (v[a] * image + g[a] * down)
        return [], tuple(out)

    return rows_loop(lo, hi, step, tuple(acc), tiles=4)


def crossing_sums(s, fx, lo, hi, acc):
    def step(r, acc):
        f = at(fx, r)
        d = [fat(s, a, r) - fat(s, a, r + CY) for a in range(K)]
        e = [f * t for t in d]
        return [], tuple(t + d[a] * e[b] for t, (a, b) in zip(acc, PAIRS))

    return rows_loop(lo, hi, step, tuple(acc), tiles=1)


def turned(scal, s, kp, first, window, tile, ptile, blocks, back=0):
    start = scal[1] - WMAX

    def step(block, row, lane):
        ptile[...] = kp[pl.ds(row, CZ), :].T
        kw = ptile[pl.ds(start, WMAX), :]
        for a in range(K):
            tile[a] = s[a, pl.ds(aligned(row - back, 8), CZ), :].T
        for a in range(K):
            u = tile[a, pl.ds(start, WMAX), :] * kw
            f = tile[a, pl.ds(0, WMAX), :]
            for t in range(WMAX):
                first[pl.ds(t * K + a, 1), pl.ds(lane, CZ)] = f[t : t + 1]
                window[pl.ds(t * K + a, 1), pl.ds(lane, CZ)] = u[t : t + 1]

    def one(block, carry):
        step(block, aligned(OFF + block * CZ, 8), aligned((block - blocks[0]) * CZ, CZ))
        return carry

    loop(blocks[0], blocks[1], one, 0)


def copy_all(pairs, sem):
    copies = [pltpu.make_async_copy(src, dst, sem.at[i]) for i, (src, dst) in enumerate(pairs)]
    for c in copies:
        c.start()
    return copies


def wait_all(copies):
    for c in copies:
        c.wait()


def pack_kernel(sv, perm, acc, down, up, sem):
    pairs = []
    for out, lo, acc_lo in ((down, 0, 0), (up, SLAB - HALO, SLAB - HALO_ACC)):
        pairs.append((sv.at[:, pl.ds(lo, HALO)], out.at[pl.ds(0, K * HALO)].reshape(K, HALO, CZ)))
        pairs.append((perm.at[pl.ds(lo, HALO)], out.at[pl.ds(K * HALO, HALO)]))
        pairs.append((acc.at[pl.ds(acc_lo, HALO_ACC)], out.at[pl.ds((K + 1) * HALO, HALO_ACC)]))
    wait_all(copy_all(pairs, sem))


INSIDE = SLAB - 4 * CY
EDGE = 2 * CY + 32
FIRST = WMAX * K
SENT = SLAB // CZ * FIRST + 8


BACK = OFF + 2 * CY
OWN = SLAB - CZ
EDGE_BACK = (OFF - 32, OFF + OWN)


def copy_rows(moves, count, group):
    def one(i, carry):
        values = []
        for j in range(group):
            for dst, at_dst, src, at_src in moves:
                rows = [pl.ds(aligned(r + (i * group + j) * 8, 8), 8) for r in (at_dst, at_src)]
                if len(dst.shape) == 2:
                    values.append((dst, (rows[0], slice(None)), src[rows[1], :]))
                else:
                    for a in range(K):
                        values.append((dst, (a, rows[0], slice(None)), src[a, rows[1], :]))
        for dst, place, value in values:
            dst[place] = value
        return carry

    assert count % (8 * group) == 0
    loop(0, count // (8 * group), one, 0)


def interior_kernel(
    scal, sv, perm, acc, si, ve, kp, ac, fx, fy, fz, w, gram, flux, first, window, v0, v1, tile, ptile, sem
):
    slab = pl.ds(OFF, SLAB)
    a, b, c = copy_all([(perm, kp.at[slab]), (acc, ac.at[slab]), (sv, v0.at[:, slab])], sem)
    a.wait()
    faces(scal, kp, fx, fy, fz, 0, SLAB - CY, 20)
    b.wait()
    weights(ac, fx, fy, fz, w, CY, SLAB - CY, 16)
    c.wait()
    smooth(scal, v0, v1, fx, fy, fz, w, CY, SLAB - CY, True)
    out = copy_all(
        [
            (v0.at[:, pl.ds(OFF, CZ)], ve.at[0]),
            (v0.at[:, pl.ds(OFF + OWN, CZ)], ve.at[1]),
            (v1.at[:, pl.ds(OFF + CY, CZ)], ve.at[2]),
            (v1.at[:, pl.ds(OFF + SLAB - CY - CZ, CZ)], ve.at[3]),
        ],
        sem,
    )
    smooth(scal, v1, si, fx, fy, fz, w, 2 * CY, SLAB - 2 * CY, False, back=BACK)
    zero = [jnp.zeros((8, CZ), F32)] * NP
    for i, t in enumerate(gram_sums(si, 2 * CY, SLAB - 2 * CY, zero, back=BACK)):
        gram[i] = t
    for i, t in enumerate(flux_sums(si, ac, fx, fy, fz, 3 * CY, SLAB - 3 * CY, zero, back=BACK)):
        flux[i] = t
    turned(scal, si, kp, first, window, tile, ptile, (1, 7), back=BACK)
    wait_all(out)


def edge_kernel(
    scal, left, right, ve, kpi, aci, fxi, fyi, fzi, wi, gram, firsti, windowi,
    se, sent, window, fx, fy, fz, v0, v1, kp, ac, w, fe, we, tile, ptile,
):
    ends = ((left, -HALO, -HALO_ACC, 0), (right, SLAB, SLAB, OWN))
    moves = [(kp, OFF + lo, src, K * HALO) for src, lo, _, _ in ends]
    copy_rows(moves, HALO, 20)
    moves = [(ac, OFF + lo, src, (K + 1) * HALO) for src, _, lo, _ in ends]
    copy_rows(moves, HALO_ACC, 12)
    copy_rows([(new, OFF + n, old, OFF + n) for new, old in ((kp, kpi), (ac, aci)) for n in (0, OWN)], CZ, 16)
    both = (0, SLAB - 4 * CY)
    copy_rows([(new, OFF + n, old, OFF + n) for new, old in ((fx, fxi), (fy, fyi), (fz, fzi)) for n in both], 3 * CY, 8)
    copy_rows([(w, OFF + n, wi, OFF + n) for n in (CY, SLAB - 2 * CY)], CY, 8)
    faces(scal, kp, fx, fy, fz, -HALO, 0, 20)
    faces(scal, kp, fx, fy, fz, SLAB - CY, SLAB + HALO_ACC, 20)
    weights(ac, fx, fy, fz, w, -HALO_ACC, CY, 20)
    weights(ac, fx, fy, fz, w, SLAB - CY, SLAB + HALO_ACC, 20)
    for src, lo, _, _ in ends:
        for a in range(K):
            copy_rows([(v0.at[a], OFF + lo, src, a * HALO)], HALO, 20)
    for i, near in enumerate((0, OWN)):
        copy_rows([(v0, OFF + near, ve.at[i], 0)], CZ, 8)
    for i, near in enumerate((CY, SLAB - CY - CZ)):
        copy_rows([(v1, OFF + near, ve.at[2 + i], 0)], CZ, 8)
    smooth(scal, v0, v1, fx, fy, fz, w, -HALO_ACC, CY, True, 20)
    smooth(scal, v0, v1, fx, fy, fz, w, SLAB - CY, SLAB + HALO_ACC, True, 20)
    smooth(scal, v1, se.at[0], fx, fy, fz, w, -32, 2 * CY, False, 20, EDGE_BACK[0])
    smooth(scal, v1, se.at[1], fx, fy, fz, w, SLAB - 2 * CY, SLAB + 32, False, 20, EDGE_BACK[1])
    window[:, pl.ds(CZ, INSIDE)] = windowi[...]
    for i in range(INSIDE // CZ):
        sent[pl.ds((i + 1) * FIRST, FIRST), :] = firsti[:, i * CZ : (i + 1) * CZ]
    for i, lane, end in ((0, 0, 0), (7, OWN, 1)):
        turned(scal, se.at[end], kp, fe, we, tile, ptile, (i, i + 1), EDGE_BACK[end])
        sent[pl.ds(i * FIRST, FIRST), :] = fe[...]
        window[:, pl.ds(lane, CZ)] = we[...]
    acc = [gram[i] for i in range(NP)]
    acc = gram_sums(se.at[0], 0, 2 * CY, acc, EDGE_BACK[0])
    acc = gram_sums(se.at[1], SLAB - 2 * CY, SLAB, acc, EDGE_BACK[1])
    lane = lanes()
    res = jnp.zeros((8, CZ), F32)
    for b, col in enumerate(lane_sums(acc)):
        res = jnp.where(lane == b, col, res)
    sent[pl.ds(SENT - 8, 8), :] = res


def flux_kernel(se, si, ac, fx, fy, fz, flux, part, s):
    acc = [flux[i] for i in range(NP)]
    copy_rows([(s, OFF - 32, se.at[0], 0), (s, OFF + OWN, se.at[1], 0)], EDGE, 4)
    copy_rows([(s, OFF + CZ, si, 0), (s, OFF + OWN - CZ, si, INSIDE - CZ)], CZ, 4)
    acc = flux_sums(s, ac, fx, fy, fz, 0, CY, acc, before=False)
    acc = flux_sums(s, ac, fx, fy, fz, CY, 3 * CY, acc)
    acc = flux_sums(s, ac, fx, fy, fz, SLAB - 3 * CY, SLAB - CY, acc)
    acc = flux_sums(s, ac, fx, fy, fz, SLAB - CY, SLAB, acc, after=False)
    acc = crossing_sums(s, fx, -32, 0, acc)
    acc = crossing_sums(s, fx, SLAB - CY, SLAB - 32, acc)
    lane = lanes()
    res = jnp.zeros((8, CZ), F32)
    for b, col in enumerate(lane_sums(acc)):
        res = jnp.where(lane == b, col, res)
    part[...] = res


def lane_sums(acc):
    row = sublanes()
    cols = []
    for b in range(K):
        x = jnp.zeros((8, CZ), F32)
        for a in range(K):
            p = PAIRS.index((min(a, b), max(a, b)))
            x = jnp.where(row == a, jnp.sum(acc[p], axis=0, keepdims=True), x)
        cols.append(jnp.sum(x, axis=1, keepdims=True))
    return cols


GRAM = NB * K
FLUX = GRAM + K
OTHERS = FLUX + K


def couple_kernel(scal, window, near, far, part, msg, chosen, prod):
    for n in range(NB):
        m = scal[8 + n] ^ scal[3]
        place = lax.shift_right_logical(m, 1)
        odd = (m & 1) == 1
        for i in range(SLAB // CZ):
            for t in range(WMAX):
                rows = pl.ds(i * FIRST + t * K, K)
                value = jnp.where(odd, far[place, rows, :], near[place, rows, :])
                chosen[pl.ds((t * NB + n) * K, K), i * CZ : (i + 1) * CZ] = value
    mine, mine_low = pieces(window[...])
    theirs, theirs_low = pieces(chosen[...])
    both = (((1,), (1,)), ((), ()))
    prod[:, : WMAX * NB * K] = (
        lax.dot_general(mine, theirs_low, both, preferred_element_type=F32)
        + lax.dot_general(mine_low, theirs, both, preferred_element_type=F32)
    ) + lax.dot_general(mine, theirs, both, preferred_element_type=F32)
    lane = lax.broadcasted_iota(jnp.int32, (8, 2 * CZ), 1)
    total = jnp.zeros((8, 2 * CZ), F32)
    for t in range(WMAX):
        x = jnp.zeros((8, 2 * CZ), F32)
        for n in range(NB):
            width = scal[16 + n]
            d = jnp.where(t < width, WMAX - width + t, 0)
            v = prod[pl.ds(pl.multiple_of(d * K, K), K), :]
            lo = (t * NB + n) * K
            keep = (lane >= lo) & (lane < lo + K) & (t < width)
            x = jnp.where(keep, v, x)
        total = total + (pltpu.roll(x, 2 * CZ - t * NB * K, 1) if t else x)
    lane = lanes()
    res = jnp.where(lane < GRAM, total[:, :CZ], 0.0)
    res = res + pltpu.roll(part[...], FLUX, 1)
    for m in range(SUBDOMAINS):
        g = (far if m & 1 else near)[m // 2, pl.ds(SENT - 8, 8), :]
        res = res + pltpu.roll(g, OTHERS + (m - 1) * K if m else GRAM, 1)
    for i in range(msg.shape[0]):
        msg[i] = res


def eliminate(grams):
    row, lane = sublanes(), lanes()
    column = row[:, :1]
    es = []
    for g in grams:
        e = jnp.where(lane < K, g, jnp.where(lane == row + K, 1.0, 0.0))
        es.append(jnp.where(lane < 2 * K, e, 0.0))
    roots = [jnp.ones((8, 1), F32)] * len(es)
    for k in range(K):
        for m, e in enumerate(es):
            pivot = e[k : k + 1, k : k + 1]
            factor = jnp.where(column > k, e[:, k : k + 1] / pivot, 0.0)
            roots[m] = jnp.where(column == k, 1.0 / jnp.sqrt(pivot), roots[m])
            es[m] = e - factor * e[k : k + 1, :]
    return [jnp.where(lane < K, pltpu.roll(e * root, CZ - K, 1), 0.0) for e, root in zip(es, roots)]


def finish_kernel(scale, scal, got, si, se, basis, galerkin, coupling, inverse, out, sem):
    total = jnp.sum(got[...], axis=0) * scale
    (li,) = eliminate([pltpu.roll(total, CZ - GRAM, 1)])
    inverse[0] = li
    c = {(b, a): jnp.broadcast_to(li[a : a + 1, b : b + 1], (8, CZ)) for b, a in PAIRS}
    copies = []
    for i in range(SLAB // CZ):
        if i == 0:
            src = se.at[0, :, pl.ds(32, CZ)]
        elif i == SLAB // CZ - 1:
            src = se.at[1, :, pl.ds(0, CZ)]
        else:
            src = si.at[:, pl.ds((i - 1) * CZ, CZ)]

        def step(j, carry, src=src, i=i):
            stores = []
            for t in range(8):
                r = pl.multiple_of(j * 64 + t * 8, 8)
                v = [src[a, pl.ds(r, 8), :] for a in range(K)]
                for a in range(K):
                    x = c[0, a] * v[0]
                    for b in range(1, a + 1):
                        x = x + c[b, a] * v[b]
                    stores.append((a, r, x))
            for a, r, x in stores:
                out[i, a, pl.ds(r, 8), :] = x
            return carry

        lax.fori_loop(0, CZ // 64, step, 0)
        copies.append(pltpu.make_async_copy(out.at[i], basis.at[:, pl.ds(i * CZ, CZ)], sem.at[i]))
        copies[-1].start()
    others = eliminate([pltpu.roll(total, CZ - OTHERS - m * K, 1) for m in range(SUBDOMAINS - 1)])
    for m, other in enumerate(others):
        inverse[m + 1] = other
    y = jnp.dot(li[:, :K], total[:, :OTHERS], precision=HIGHEST, preferred_element_type=F32)
    transposed = (((1,), (1,)), ((), ()))
    galerkin[...] = lax.dot_general(
        y[:, FLUX:OTHERS], li[:, :K], transposed, precision=HIGHEST, preferred_element_type=F32
    )
    for n in range(NB):
        other = inverse[scal[8 + n] ^ scal[3]]
        coupling[n] = lax.dot_general(
            y[:, n * K : n * K + K], other[:, :K], transposed, precision=HIGHEST, preferred_element_type=F32
        )
    wait_all(copies)


def params(mib=40):
    return pltpu.CompilerParams(vmem_limit_bytes=mib * 1024 * 1024)


def cost(us):
    return pl.CostEstimate(flops=0, bytes_accessed=int(us * 3.0e6), transcendentals=0)


def swap(x, bits):
    return lax.ppermute(x, "subdomai", [(i, i ^ bits) for i in range(lax.axis_size("subdomai"))])


def body(start_vectors, permeability, accumulation, extents, neighbour_ids, intersection_widths):
    groups = lax.axis_size("inner")
    cells = groups * SLAB * CZ
    inner = lax.axis_index("inner")
    own = lax.axis_index("subdomai")
    sv = start_vectors.reshape(K, SLAB, CZ)
    perm = permeability.reshape(SLAB, CZ)
    acc = accumulation.reshape(SLAB, CZ)
    scal = jnp.concatenate(
        [
            extents[0],
            jnp.stack([inner * 16, own]).astype(jnp.int32),
            jnp.zeros(4, jnp.int32),
            neighbour_ids[0],
            jnp.zeros(2, jnp.int32),
            intersection_widths[0],
            jnp.zeros(10, jnp.int32),
        ]
    )
    down, up = pl.pallas_call(
        pack_kernel,
        out_shape=(shape(PACK, CZ),) * 2,
        in_specs=[HBM] * 3,
        out_specs=(VMEM,) * 2,
        scratch_shapes=[pltpu.SemaphoreType.DMA((6,))],
        compiler_params=params(60),
        name="pack",
    )(sv, perm, acc)
    right = lax.ppermute(down, "inner", [(i, (i - 1) % groups) for i in range(groups)])
    left = lax.ppermute(up, "inner", [(i, (i + 1) % groups) for i in range(groups)])
    field, plain = pltpu.VMEM((K, RT, CZ), F32), pltpu.VMEM((RT, CZ), F32)
    turning = [pltpu.VMEM((K, CZ, CZ), F32), pltpu.VMEM((CZ, CZ), F32)]
    turn = shape(FIRST, INSIDE)
    si, ve, kp, ac, fx, fy, fz, w, gram, flux, first, window = pl.pallas_call(
        interior_kernel,
        out_shape=(shape(K, INSIDE, CZ), shape(4, K, CZ, CZ))
        + (shape(RT, CZ),) * 6
        + (shape(NP, 8, CZ),) * 2
        + (turn,) * 2,
        in_specs=[SMEM, HBM, HBM, HBM],
        out_specs=(VMEM,) * 12,
        scratch_shapes=[field] * 2 + turning + [pltpu.SemaphoreType.DMA((4,))],
        compiler_params=params(36),
        cost_estimate=cost(15),
        name="interior",
    )(scal, sv, perm, acc)
    se, sent, window, fxe, fye, fze = pl.pallas_call(
        edge_kernel,
        out_shape=(shape(2, K, EDGE, CZ), shape(SENT, CZ), shape(FIRST, SLAB)) + (shape(RT, CZ),) * 3,
        in_specs=[SMEM] + [VMEM] * 12,
        out_specs=(VMEM,) * 6,
        scratch_shapes=[field] * 2 + [plain] * 3 + [pltpu.VMEM((FIRST, CZ), F32)] * 2 + turning,
        compiler_params=params(24),
        cost_estimate=cost(6),
        name="edge",
    )(scal, left, right, ve, kp, ac, fx, fy, fz, w, gram, first, window)
    moved = [swap(sent, bits) for bits in (2, 6, 4)]
    part = pl.pallas_call(
        flux_kernel,
        out_shape=shape(8, CZ),
        in_specs=[VMEM] * 7,
        out_specs=VMEM,
        scratch_shapes=[field],
        compiler_params=params(10),
        cost_estimate=cost(3),
        name="flux",
    )(se, si, ac, fxe, fye, fze, flux)
    moved, part = lax.optimization_barrier((moved, part))
    near = jnp.stack([sent, moved[0], moved[2], moved[1]])
    far = swap(near, 1)
    msg = pl.pallas_call(
        couple_kernel,
        out_shape=shape(groups, 8, CZ),
        in_specs=[SMEM] + [VMEM] * 4,
        out_specs=VMEM,
        scratch_shapes=[pltpu.VMEM((WMAX * NB * K, SLAB), F32), pltpu.VMEM((FIRST, 2 * CZ), F32)],
        compiler_params=params(8),
        cost_estimate=cost(1),
        name="couple",
    )(scal, window, near, far, part)
    got = lax.all_to_all(msg, "inner", 0, 0)
    basis, galerkin, coupling = pl.pallas_call(
        functools.partial(finish_kernel, 1.0 / cells),
        out_shape=(shape(K, SLAB, CZ), shape(K, K), shape(NB, K, K)),
        in_specs=[SMEM] + [VMEM] * 3,
        out_specs=(HBM, VMEM, VMEM),
        scratch_shapes=[
            pltpu.VMEM((SUBDOMAINS, 8, CZ), F32),
            pltpu.VMEM((SLAB // CZ, K, CZ, CZ), F32),
            pltpu.SemaphoreType.DMA((SLAB // CZ,)),
        ],
        compiler_params=params(8),
        cost_estimate=cost(5),
        name="finish",
    )(scal, got, si, se)
    return basis.reshape(start_vectors.shape), galerkin[None], coupling[None]


def solution(mesh):
    return jax.shard_map(
        body,
        mesh=mesh,
        in_specs=(
            P(None, ("subdomai", "inner"), None, None),
            P(("subdomai", "inner"), None, None),
            P(("subdomai", "inner"), None, None),
            P("subdomai", None),
            P("subdomai", None),
            P("subdomai", None),
        ),
        out_specs=(
            P(None, ("subdomai", "inner"), None, None),
            P("subdomai", None, None),
            P("subdomai", None, None, None),
        ),
        check_vma=False,
    )
```
